512 devices in a mesh: view: 64 (over x_lo, z, core), strip: 8 (over y, x_hi).
Axes of the slice: x: 4 (x_hi: 2, x_lo: 2; x = x_hi * 2 + x_lo), y: 4, z: 16, core: 2. Of those that a mesh axis runs over, the one named last changes fastest.
Arguments:
- slab: bfloat16 [64, 2, 128, 1024], P('view', None, None, 'strip'), may hold values from -6 to 6
- psi_start: float32 [64, 2, 128, 1024], P('view', None, None, 'strip'), may hold values from -6 to 6
- dual: float32 [64, 2, 128, 1024], P('view', None, None, 'strip'), may hold values from -3 to 3
- amplitudes: float32 [64, 32, 128, 128], P('view', 'strip'), may hold values from 0.2 to 3
- offsets: int32 [64, 32], P('view', 'strip'), may hold values from 0 to 127
- angles: int32 [64], replicated, may hold values from 0 to 32
- probe: float32 [2, 128, 128], replicated, may hold values from -6 to 6
Outputs:
- psi_out: float32 [64, 2, 128, 1024], P('view', None, None, 'strip')
- slab_out: bfloat16 [64, 2, 128, 1024], P('view', None, None, 'strip')
The draws below stay inside these ranges and needn't reach their ends.
Inputs may be any that keep to these rules, and one draw needn't show every extreme that they name: offsets lie inside the strip of their position.
All inputs are finite; a program needn't handle non-finite values.
Results may differ from the reference program's by a relative error of at most 0.0047.
Values may be sent and summed in bfloat16 or wider, within the bound.
No kernel may reach another device: no remote copies, remote signals or barrier semaphores. Data moves between devices by JAX's collectives and lax.ppermute only.
A program may use at most 64 MiB of HBM per device.

```python
import math
import jax
import jax.numpy as jnp
from jax import lax

W = 1024
PATCH = 128
HALO = 16
POS_DEV = 4
ITERS = 2
VIEWS = 64
Z = 64
H = 128
STRIP_W = 128
NPOS = 32
N_STRIP = 8


def plant(array, rng, least, top_value):
    longest = array.shape.index(max(array.shape))
    spots = []
    for shift in (0, 1):
        where = [jax.random.randint(jax.random.fold_in(rng, axis), (), 0, length) for axis, length in enumerate(array.shape)]
        where[longest] = (where[longest] + shift) % array.shape[longest]
        spots.append(tuple(where))
    return array.at[spots[0]].set(least).at[spots[1]].set(top_value)


def levels(key, extent, split, least, top_value):
    def one(axis_at, blocks):
        draws = jax.random.uniform(jax.random.fold_in(jax.random.fold_in(key, 6), axis_at), (blocks,), jnp.float32, least / len(split), top_value / len(split))
        return jnp.repeat(jnp.exp(draws), extent[axis_at] // blocks).reshape((-1,) + (1,) * (len(extent) - axis_at - 1))

    loudness = one(*split[0])
    for cut in split[1:]:
        loudness = loudness * one(*cut)
    return loudness


def bell_draw(stream_key, extent, scale, reach, cuts=(), held_as=jnp.bfloat16):
    array = jax.random.normal(stream_key, extent, jnp.float32) * scale
    if len(cuts) > 0:
        array = levels(stream_key, extent, cuts, -0.22, 0.18) * array
    return jnp.clip(array, min=-reach, max=reach).astype(held_as)


def setup_inputs(seed: int = 0) -> dict:
    key_of = jax.random.split(jax.random.key(seed), 8)
    return {
        "slab": bell_draw(key_of[0], (Z, 2, H, W), 1.0, 6.0, ((0, 64), (3, 8))),
        "psi_start": bell_draw(key_of[1], (VIEWS, 2, H, W), 1.0, 6.0, ((0, 64), (3, 8)), jnp.float32),
        "dual": bell_draw(key_of[2], (VIEWS, 2, H, W), 0.5, 3.0, ((0, 64), (3, 8)), jnp.float32),
        "amplitudes": jnp.clip(jnp.exp(math.log(3.0) - 2.7080502 * jax.random.uniform(key_of[3], (VIEWS, NPOS, PATCH, PATCH), jnp.float32) ** levels(key_of[3], (VIEWS, NPOS, PATCH, PATCH), ((0, 64), (1, 8)), -0.2, 0.2)), 0.2, 3.0),
        "offsets": plant(jax.random.randint(key_of[4], (VIEWS, NPOS), 0, W // N_STRIP), jax.random.fold_in(key_of[4], 1), 0, (W // N_STRIP) - 1).astype(jnp.int32),
        "angles": plant(jax.random.randint(key_of[5], (VIEWS,), 0, 2 * HALO + 1), jax.random.fold_in(key_of[5], 1), 0, 2 * HALO).astype(jnp.int32),
        "probe": bell_draw(key_of[6], (2, PATCH, PATCH), 1.0, 6.0, (), jnp.float32),
    }


coupling = 0.5
descent = 0.5

def shear_shift(tilt, depth):
    return tilt * (2 * depth - Z + 1) // Z

def reference(slab, psi_start, dual, amplitudes, offsets, angles, probe):
    volume = slab.astype(jnp.float32)
    padded = jnp.pad(volume, ((0, 0), (0, 0), (0, 0), (HALO, HALO)))
    depths = jnp.arange(Z, dtype=jnp.int32)
    tilts = (angles - HALO).astype(jnp.int32)

    def project(tilt):
        shifts = shear_shift(tilt, depths).astype(jnp.int32)
        pieces = jax.vmap(lambda layer, amount: lax.dynamic_slice_in_dim(layer, (HALO + amount).astype(jnp.int32), W, 2))(padded, shifts)
        return lax.optimization_barrier(jnp.sum(pieces, axis=0)) / math.sqrt(Z)
    projections = lax.map(project, tilts)
    probe_c = lax.complex(probe[0], probe[1])
    strip_base = (jnp.arange(NPOS, dtype=jnp.int32) // POS_DEV * STRIP_W).astype(jnp.int32)

    def ptycho(items):
        psi_view, proj_view, dual_view, amps_view, offs_view = items
        columns = (strip_base + offs_view).astype(jnp.int32)
        index_table = columns[:, None] + jnp.arange(PATCH, dtype=jnp.int32)[None, :]
        current = psi_view
        for sweep in range(ITERS):
            obj = lax.complex(current[0], current[1])
            extended = jnp.pad(obj, ((0, 0), (0, STRIP_W)))
            patches = jax.vmap(lambda begin: lax.dynamic_slice_in_dim(extended, begin, PATCH, 1))(columns)
            exitw = probe_c * patches
            far = jnp.fft.fft2(exitw, norm='ortho')
            fixed = amps_view * far / jnp.sqrt(jnp.real(far) ** 2 + jnp.imag(far) ** 2 + 1.0)
            back = jnp.fft.ifft2(fixed, norm='ortho')
            grad = jnp.conj(probe_c) * (back - exitw)
            spread = jnp.zeros((H, W + STRIP_W), grad.dtype).at[:, index_table].add(jnp.transpose(grad, (1, 0, 2)))
            update = jnp.stack([jnp.real(spread), jnp.imag(spread)])[:, :, :W]
            current = current + update / POS_DEV + coupling * (proj_view - dual_view - current)
        return current
    psi_out = lax.map(ptycho, (psi_start, projections, dual, amplitudes, offsets))
    rounded = (projections - psi_out - dual).astype(jnp.bfloat16)
    rounded = lax.optimization_barrier(rounded)
    residual = rounded.astype(jnp.float32)
    rpad = jnp.pad(residual, ((0, 0), (0, 0), (0, 0), (HALO, HALO)))

    def backproject(depth):
        shifts = shear_shift(tilts, depth).astype(jnp.int32)
        pieces = jax.vmap(lambda layer, amount: lax.dynamic_slice_in_dim(layer, (HALO - amount).astype(jnp.int32), W, 2))(rpad, shifts)
        return lax.optimization_barrier(jnp.sum(pieces, axis=0)) / math.sqrt(Z)
    grads = lax.map(backproject, depths)
    slab_out = (volume - descent * grads).astype(jnp.bfloat16)
    return (psi_out, slab_out)
```

```python
import math

import jax
import jax.numpy as jnp
import numpy as np
from jax import lax
from jax.experimental import pallas as pl
from jax.experimental.pallas import tpu as pltpu
from jax.sharding import PartitionSpec as P

HALO = 16
ITERS = 2
TAPS = 2 * HALO + 1
coupling = 0.5
descent = 0.5
bf16 = jnp.bfloat16
f32 = jnp.float32


def dft_blocks(length):
    counter = np.arange(length)
    phase = (counter[:, None] * counter[None, :]) % length
    angle = phase.astype(np.float64) * (2.0 * math.pi / length)
    cosine = np.cos(angle) / math.sqrt(length)
    sine = np.sin(angle) / math.sqrt(length)
    ahead = np.block([[cosine, sine], [-sine, cosine]])
    behind = np.block([[cosine, -sine], [sine, cosine]])
    both = np.stack([ahead, behind]).astype(np.float32)
    high = both.astype(jnp.bfloat16)
    low = (both - high.astype(np.float32)).astype(jnp.bfloat16)
    return jnp.asarray(np.stack([high, low], axis=1))


def split(value):
    high = value.astype(bf16)
    low = (value - high.astype(f32)).astype(bf16)
    return high, low


def dot(a, b):
    return jnp.dot(a, b, preferred_element_type=f32)


def table_left(table, value):
    high, low = split(value)
    return dot(table[0], high) + dot(table[0], low) + dot(table[1], high)


def table_right(value, table):
    high, low = split(value)
    return dot(high, table[0]) + dot(low, table[0]) + dot(high, table[1])


def gradient_kernel(starts, own, following, measured, probe, tables, spread):
    side = own.shape[1]
    count = measured.shape[0]
    ahead = (tables[0, 0], tables[0, 1])
    behind = (tables[1, 0], tables[1, 1])
    wide_real = jnp.concatenate([own[0], following[0]], axis=1)
    wide_imag = jnp.concatenate([own[1], following[1]], axis=1)
    probe_real = probe[0]
    probe_imag = probe[1]
    exits = []
    for p in range(count):
        by = lax.rem(2 * side - starts[p], 2 * side)
        patch_real = pltpu.roll(wide_real, by, 1)[:, :side]
        patch_imag = pltpu.roll(wide_imag, by, 1)[:, :side]
        exit_real = probe_real * patch_real - probe_imag * patch_imag
        exit_imag = probe_real * patch_imag + probe_imag * patch_real
        exits.append(jnp.concatenate([exit_real, exit_imag], axis=0))
    exitw = jnp.concatenate(exits, axis=1)
    left = table_left(ahead, exitw)

    def to_rows(value):
        return jnp.concatenate(
            [
                jnp.concatenate(
                    [
                        value[:side, p * side : (p + 1) * side],
                        value[side:, p * side : (p + 1) * side],
                    ],
                    axis=1,
                )
                for p in range(count)
            ],
            axis=0,
        )

    def to_columns(value):
        return jnp.concatenate(
            [
                jnp.concatenate(
                    [
                        value[p * side : (p + 1) * side, :side],
                        value[p * side : (p + 1) * side, side:],
                    ],
                    axis=0,
                )
                for p in range(count)
            ],
            axis=1,
        )

    far = table_right(to_rows(left), behind)
    far_real = far[:, :side]
    far_imag = far[:, side:]
    level = jnp.concatenate([measured[p] for p in range(count)], axis=0)
    factor = level * lax.rsqrt(far_real * far_real + far_imag * far_imag + 1.0)
    fixed = jnp.concatenate([far_real * factor, far_imag * factor], axis=1)
    back = table_left(behind, to_columns(table_right(fixed, ahead)))
    delta = back - exitw
    total_real = jnp.zeros((side, 2 * side), f32)
    total_imag = jnp.zeros((side, 2 * side), f32)
    nothing = jnp.zeros((side, side), f32)
    for p in range(count):
        delta_real = delta[:side, p * side : (p + 1) * side]
        delta_imag = delta[side:, p * side : (p + 1) * side]
        grad_real = probe_real * delta_real + probe_imag * delta_imag
        grad_imag = probe_real * delta_imag - probe_imag * delta_real
        total_real += pltpu.roll(jnp.concatenate([grad_real, nothing], axis=1), starts[p], 1)
        total_imag += pltpu.roll(jnp.concatenate([grad_imag, nothing], axis=1), starts[p], 1)
    spread[0, 0] = total_real[:, :side]
    spread[0, 1] = total_imag[:, :side]
    spread[1, 0] = total_real[:, side:]
    spread[1, 1] = total_imag[:, side:]


def gradient(starts, own, following, measured, probe, tables):
    vmem = pl.BlockSpec(memory_space=pltpu.VMEM)
    return pl.pallas_call(
        gradient_kernel,
        out_shape=jax.ShapeDtypeStruct((2,) + own.shape, f32),
        in_specs=[pl.BlockSpec(memory_space=pltpu.SMEM)] + [vmem] * 5,
        out_specs=vmem,
        compiler_params=pltpu.CompilerParams(vmem_limit_bytes=32 * 1024 * 1024),
    )(starts, own, following, measured, probe, tables)


def shear_kernel(scale, lines, source, choice, out, plain, taps, result):
    channels = choice.shape[0]
    side = source.shape[1]
    plain[...] = source[...].astype(f32)
    for r in range(lines):
        near = plain[pl.ds(r, channels, stride=2 * lines), :]
        edge = plain[pl.ds(lines + r, channels, stride=2 * lines), :]
        wide = jnp.concatenate([near, edge], axis=1)
        for d in range(TAPS):
            moved = pltpu.roll(wide, (2 * side + HALO - d) % (2 * side), 1)[:, :side]
            taps[d * channels : (d + 1) * channels, r * side : (r + 1) * side] = moved.astype(bf16)
    summed = dot(choice[...], taps[...]) * scale
    for r in range(lines):
        result[pl.ds(r, channels, stride=lines), :] = summed[:, r * side : (r + 1) * side]
    out[...] = result[...].astype(bf16)


def shear_sum(source, choice, scale):
    channels = choice.shape[0]
    side = source.shape[1]
    lines = source.shape[0] // (2 * channels)
    vmem = pl.BlockSpec(memory_space=pltpu.VMEM)
    return pl.pallas_call(
        lambda *refs: shear_kernel(scale, lines, *refs),
        out_shape=jax.ShapeDtypeStruct((lines * channels, side), bf16),
        in_specs=[vmem] * 2,
        out_specs=vmem,
        scratch_shapes=[
            pltpu.VMEM((2 * lines * channels, side), f32),
            pltpu.VMEM((TAPS * channels, lines * side), bf16),
            pltpu.VMEM((lines * channels, side), f32),
        ],
        compiler_params=pltpu.CompilerParams(vmem_limit_bytes=32 * 1024 * 1024),
    )(source, choice)


def strip_move(value, by):
    length = lax.axis_size("strip")
    pairs = [(i, i + by) for i in range(length) if 0 <= i + by < length]
    return lax.ppermute(value, "strip", pairs)


def with_edges(value, before, after):
    lane = lax.broadcasted_iota(jnp.int32, value.shape, value.ndim - 1)
    return jnp.where(lane < value.shape[-1] // 2, after, before)


def exchange(own, edge, groups):
    side = own.shape[-1]
    lines = own.size // (groups * side)
    parcel = jnp.concatenate(
        [own.reshape(groups, lines, side), edge.reshape(groups, lines, side)], axis=1
    )
    got = lax.all_to_all(parcel, "view", 0, 0, tiled=True)
    return got.reshape(groups * 2 * lines, side)


def give_back(value, groups):
    side = value.shape[-1]
    parcel = value.reshape(groups, value.shape[0] // groups, side)
    return lax.all_to_all(parcel, "view", 0, 0, tiled=True)


def per_device(slab, psi_start, dual, amplitudes, offsets, angles, probe):
    slices = lax.axis_size("view")
    own_slab = slab[0]
    shape = own_slab.shape
    psi = psi_start[0]
    own_dual = dual[0]
    measured = amplitudes[0]
    starts = offsets[0]
    root_scale = 1.0 / math.sqrt(slices)
    tables = dft_blocks(probe.shape[1])
    step_size = 1.0 / starts.shape[0]

    depth = jnp.arange(slices, dtype=jnp.int32)
    tilt = angles - HALO
    shift = (tilt[:, None] * (2 * depth[None, :] - slices + 1)) // slices
    tap = jnp.arange(TAPS, dtype=jnp.int32) - HALO
    choice_project = (
        (shift[:, None, :] == tap[None, :, None]).astype(bf16).reshape(slices, TAPS * slices)
    )
    choice_back = (
        (-shift.T[:, None, :] == tap[None, :, None]).astype(bf16).reshape(slices, TAPS * slices)
    )

    slab_edge = with_edges(own_slab, strip_move(own_slab, 1), strip_move(own_slab, -1))
    following = strip_move(psi, -1)
    lined = exchange(own_slab, slab_edge, slices)
    spread = gradient(starts, psi, following, measured, probe, tables)
    spill = strip_move(spread[1], 1)
    sums = shear_sum(lined, choice_project, root_scale)
    projected = give_back(sums, slices).reshape(shape).astype(f32)
    pull = projected - own_dual
    psi = psi + step_size * (spread[0] + spill) + coupling * (pull - psi)

    following = strip_move(psi, -1)
    spread = gradient(starts, psi, following, measured, probe, tables)
    part = psi + step_size * spread[0] + coupling * (pull - psi)
    rest = (pull - part).astype(bf16)
    outer = (spread[1] * step_size).astype(bf16)
    up = strip_move(jnp.stack([rest, outer]), 1)
    up_two = strip_move(outer, 2)
    down = strip_move(rest, -1)
    incoming = up[1].astype(f32)
    psi = part + incoming
    residual = (pull - psi).astype(bf16)
    residual_edge = with_edges(
        residual,
        (up[0].astype(f32) - up_two.astype(f32)).astype(bf16),
        (down.astype(f32) - outer.astype(f32)).astype(bf16),
    )
    last = lax.axis_index("strip") == lax.axis_size("strip") - 1
    first = lax.axis_index("strip") == 0
    lane = lax.broadcasted_iota(jnp.int32, shape, 2)
    outside = (last & (lane < shape[2] // 2)) | (first & (lane >= shape[2] // 2))
    residual_edge = jnp.where(outside, jnp.zeros_like(residual_edge), residual_edge)
    lined = exchange(residual, residual_edge, slices)
    sums = shear_sum(lined, choice_back, descent * root_scale)
    backward = give_back(sums, slices).reshape(shape).astype(f32)
    slab_new = (own_slab.astype(f32) - backward).astype(bf16)
    return (psi[None], slab_new[None])


def solution(mesh):
    return jax.shard_map(
        per_device,
        mesh=mesh,
        in_specs=(
            P("view", None, None, "strip"),
            P("view", None, None, "strip"),
            P("view", None, None, "strip"),
            P("view", "strip", None, None),
            P("view", "strip"),
            P(),
            P(),
        ),
        out_specs=(P("view", None, None, "strip"), P("view", None, None, "strip")),
        check_vma=False,
    )
```

```python
import math

import jax
import jax.numpy as jnp
import numpy as np
from jax import lax
from jax.experimental import pallas as pl
from jax.experimental.pallas import tpu as pltpu
from jax.sharding import PartitionSpec as P

HALO = 16
ITERS = 2
TAPS = 2 * HALO + 1
coupling = 0.5
descent = 0.5
bf16 = jnp.bfloat16
f32 = jnp.float32


def dft_blocks(length):
    counter = np.arange(length)
    phase = (counter[:, None] * counter[None, :]) % length
    angle = phase.astype(np.float64) * (2.0 * math.pi / length)
    cosine = np.cos(angle) / math.sqrt(length)
    sine = np.sin(angle) / math.sqrt(length)
    ahead = np.block([[cosine, sine], [-sine, cosine]])
    behind = np.block([[cosine, -sine], [sine, cosine]])
    both = np.stack([ahead, behind]).astype(np.float32)
    high = both.astype(jnp.bfloat16)
    low = (both - high.astype(np.float32)).astype(jnp.bfloat16)
    return jnp.asarray(np.stack([high, low], axis=1))


def split(value):
    high = value.astype(bf16)
    low = (value - high.astype(f32)).astype(bf16)
    return high, low


def dot(a, b):
    return jnp.dot(a, b, preferred_element_type=f32)


def table_left(table, value):
    high, low = split(value)
    return dot(table[0], high) + dot(table[0], low) + dot(table[1], high)


def table_right(value, table):
    high, low = split(value)
    return dot(high, table[0]) + dot(low, table[0]) + dot(high, table[1])


def gradient_kernel(starts, own, following, measured, probe, tables, spread):
    side = own.shape[1]
    count = measured.shape[0]
    ahead = (tables[0, 0], tables[0, 1])
    behind = (tables[1, 0], tables[1, 1])
    wide_real = jnp.concatenate([own[0], following[0]], axis=1)
    wide_imag = jnp.concatenate([own[1], following[1]], axis=1)
    probe_real = probe[0]
    probe_imag = probe[1]
    exits = []
    for p in range(count):
        by = lax.rem(2 * side - starts[p], 2 * side)
        patch_real = pltpu.roll(wide_real, by, 1)[:, :side]
        patch_imag = pltpu.roll(wide_imag, by, 1)[:, :side]
        exit_real = probe_real * patch_real - probe_imag * patch_imag
        exit_imag = probe_real * patch_imag + probe_imag * patch_real
        exits.append(jnp.concatenate([exit_real, exit_imag], axis=0))
    exitw = jnp.concatenate(exits, axis=1)
    left = table_left(ahead, exitw)

    def to_rows(value):
        return jnp.concatenate(
            [
                jnp.concatenate(
                    [
                        value[:side, p * side : (p + 1) * side],
                        value[side:, p * side : (p + 1) * side],
                    ],
                    axis=1,
                )
                for p in range(count)
            ],
            axis=0,
        )

    def to_columns(value):
        return jnp.concatenate(
            [
                jnp.concatenate(
                    [
                        value[p * side : (p + 1) * side, :side],
                        value[p * side : (p + 1) * side, side:],
                    ],
                    axis=0,
                )
                for p in range(count)
            ],
            axis=1,
        )

    far = table_right(to_rows(left), behind)
    far_real = far[:, :side]
    far_imag = far[:, side:]
    level = jnp.concatenate([measured[p] for p in range(count)], axis=0)
    factor = level * lax.rsqrt(far_real * far_real + far_imag * far_imag + 1.0)
    fixed = jnp.concatenate([far_real * factor, far_imag * factor], axis=1)
    back = table_left(behind, to_columns(table_right(fixed, ahead)))
    delta = back - exitw
    total_real = jnp.zeros((side, 2 * side), f32)
    total_imag = jnp.zeros((side, 2 * side), f32)
    nothing = jnp.zeros((side, side), f32)
    for p in range(count):
        delta_real = delta[:side, p * side : (p + 1) * side]
        delta_imag = delta[side:, p * side : (p + 1) * side]
        grad_real = probe_real * delta_real + probe_imag * delta_imag
        grad_imag = probe_real * delta_imag - probe_imag * delta_real
        total_real += pltpu.roll(jnp.concatenate([grad_real, nothing], axis=1), starts[p], 1)
        total_imag += pltpu.roll(jnp.concatenate([grad_imag, nothing], axis=1), starts[p], 1)
    spread[0, 0] = total_real[:, :side]
    spread[0, 1] = total_imag[:, :side]
    spread[1, 0] = total_real[:, side:]
    spread[1, 1] = total_imag[:, side:]


def gradient(starts, own, following, measured, probe, tables):
    vmem = pl.BlockSpec(memory_space=pltpu.VMEM)
    return pl.pallas_call(
        gradient_kernel,
        out_shape=jax.ShapeDtypeStruct((2,) + own.shape, f32),
        in_specs=[pl.BlockSpec(memory_space=pltpu.SMEM)] + [vmem] * 5,
        out_specs=vmem,
        compiler_params=pltpu.CompilerParams(vmem_limit_bytes=32 * 1024 * 1024),
    )(starts, own, following, measured, probe, tables)


def shear_kernel(scale, lines, into, source, choice, out, plain, taps, result):
    channels = choice.shape[0]
    side = source.shape[1]
    pieces = source.shape[0] // (lines * channels)
    span = into * side
    plain[...] = source[...].astype(f32)
    for r in range(lines):
        near = plain[pl.ds(r, channels, stride=pieces * lines), :]
        if pieces == 1:
            edge = jnp.zeros_like(near)
        else:
            edge = plain[pl.ds(lines + r, channels, stride=pieces * lines), :]
        wide = jnp.concatenate([near, edge], axis=1)
        for d in range(TAPS):
            moved = pltpu.roll(wide, (2 * side + HALO - d) % (2 * side), 1)[:, :span]
            taps[d * channels : (d + 1) * channels, r * span : (r + 1) * span] = moved.astype(bf16)
    summed = dot(choice[...], taps[...]) * scale
    for r in range(lines):
        for j in range(into):
            begin = r * span + j * side
            result[pl.ds(j * lines + r, channels, stride=into * lines), :] = summed[
                :, begin : begin + side
            ]
    out[...] = result[...].astype(bf16)


def shear_sum(source, choice, scale, lines, into):
    channels = choice.shape[0]
    side = source.shape[1]
    pieces = source.shape[0] // (lines * channels)
    vmem = pl.BlockSpec(memory_space=pltpu.VMEM)
    return pl.pallas_call(
        lambda *refs: shear_kernel(scale, lines, into, *refs),
        out_shape=jax.ShapeDtypeStruct((into * lines * channels, side), bf16),
        in_specs=[vmem] * 2,
        out_specs=vmem,
        scratch_shapes=[
            pltpu.VMEM((pieces * lines * channels, side), f32),
            pltpu.VMEM((TAPS * channels, into * lines * side), bf16),
            pltpu.VMEM((into * lines * channels, side), f32),
        ],
        compiler_params=pltpu.CompilerParams(vmem_limit_bytes=32 * 1024 * 1024),
    )(source, choice)


def strip_move(value, by):
    length = lax.axis_size("strip")
    pairs = [(i, i + by) for i in range(length) if 0 <= i + by < length]
    return lax.ppermute(value, "strip", pairs)


def with_edges(value, before, after):
    lane = lax.broadcasted_iota(jnp.int32, value.shape, value.ndim - 1)
    return jnp.where(lane < value.shape[-1] // 2, after, before)


def exchange(parts, groups):
    side = parts[0].shape[-1]
    lines = parts[0].size // (groups * side)
    parcel = jnp.concatenate([part.reshape(groups, lines, side) for part in parts], axis=1)
    got = lax.all_to_all(parcel, "view", 0, 0, tiled=True)
    return got.reshape(groups * len(parts) * lines, side)


def give_back(value, groups):
    side = value.shape[-1]
    parcel = value.reshape(groups, value.shape[0] // groups, side)
    return lax.all_to_all(parcel, "view", 0, 0, tiled=True)


def per_device(slab, psi_start, dual, amplitudes, offsets, angles, probe):
    slices = lax.axis_size("view")
    own_slab = slab[0]
    shape = own_slab.shape
    psi = psi_start[0]
    own_dual = dual[0]
    measured = amplitudes[0]
    starts = offsets[0]
    root_scale = 1.0 / math.sqrt(slices)
    tables = dft_blocks(probe.shape[1])
    step_size = 1.0 / starts.shape[0]

    depth = jnp.arange(slices, dtype=jnp.int32)
    tilt = angles - HALO
    shift = (tilt[:, None] * (2 * depth[None, :] - slices + 1)) // slices
    tap = jnp.arange(TAPS, dtype=jnp.int32) - HALO
    choice_project = (
        (shift[:, None, :] == tap[None, :, None]).astype(bf16).reshape(slices, TAPS * slices)
    )
    choice_back = (
        (-shift.T[:, None, :] == tap[None, :, None]).astype(bf16).reshape(slices, TAPS * slices)
    )

    lines = shape[0] * shape[1] // slices
    last = lax.axis_index("strip") == lax.axis_size("strip") - 1
    first = lax.axis_index("strip") == 0
    following = strip_move(psi, -1)
    lined = exchange([own_slab], slices)
    spread = gradient(starts, psi, following, measured, probe, tables)
    sums = shear_sum(lined, choice_project, root_scale, lines, 2)
    sums, spread = lax.optimization_barrier((sums, spread))
    spill = strip_move(spread[1], 1)
    sums = give_back(sums, slices)
    projected = sums[:, :lines].reshape(shape).astype(f32)
    beyond = sums[:, lines:].reshape(shape)
    pull = projected - own_dual
    psi = psi + step_size * (spread[0] + spill) + coupling * (pull - psi)

    beyond_up = strip_move(beyond, 1)
    beyond_two = strip_move(beyond, -2)
    down = strip_move(jnp.stack([psi.astype(bf16), beyond]), -1)
    gain = with_edges(beyond, down[1], beyond_up).astype(f32)
    pull = pull + gain
    psi = psi + coupling * gain
    following = down[0].astype(f32) + coupling * with_edges(
        beyond, beyond_two, beyond
    ).astype(f32)
    following = jnp.where(last, 0.0, following)
    spread = gradient(starts, psi, following, measured, probe, tables)
    part = psi + step_size * spread[0] + coupling * (pull - psi)
    rest = (pull - part).astype(bf16)
    outer = (spread[1] * step_size).astype(bf16)
    up = strip_move(jnp.stack([rest, outer]), 1)
    up_two = strip_move(outer, 2)
    down = strip_move(rest, -1)
    incoming = up[1].astype(f32)
    psi = part + incoming
    residual = (pull - psi).astype(bf16)
    residual_edge = with_edges(
        residual,
        (up[0].astype(f32) - up_two.astype(f32)).astype(bf16),
        (down.astype(f32) - outer.astype(f32)).astype(bf16),
    )
    lane = lax.broadcasted_iota(jnp.int32, shape, 2)
    outside = (last & (lane < shape[2] // 2)) | (first & (lane >= shape[2] // 2))
    residual_edge = jnp.where(outside, jnp.zeros_like(residual_edge), residual_edge)
    lined = exchange([residual, residual_edge], slices)
    sums = shear_sum(lined, choice_back, descent * root_scale, lines, 1)
    backward = give_back(sums, slices).reshape(shape).astype(f32)
    slab_new = (own_slab.astype(f32) - backward).astype(bf16)
    return (psi[None], slab_new[None])


def solution(mesh):
    return jax.shard_map(
        per_device,
        mesh=mesh,
        in_specs=(
            P("view", None, None, "strip"),
            P("view", None, None, "strip"),
            P("view", None, None, "strip"),
            P("view", "strip", None, None),
            P("view", "strip"),
            P(),
            P(),
        ),
        out_specs=(P("view", None, None, "strip"), P("view", None, None, "strip")),
        check_vma=False,
    )
```

```python
import math

import jax
import jax.numpy as jnp
import numpy as np
from jax import lax
from jax.experimental import pallas as pl
from jax.experimental.pallas import tpu as pltpu
from jax.sharding import PartitionSpec as P

HALO = 16
ITERS = 2
TAPS = 2 * HALO + 1
coupling = 0.5
descent = 0.5
bf16 = jnp.bfloat16
f32 = jnp.float32


def dft_blocks(length):
    counter = np.arange(length)
    phase = (counter[:, None] * counter[None, :]) % length
    angle = phase.astype(np.float64) * (2.0 * math.pi / length)
    cosine = np.cos(angle) / math.sqrt(length)
    sine = np.sin(angle) / math.sqrt(length)
    ahead = np.block([[cosine, sine], [-sine, cosine]])
    behind = np.block([[cosine, -sine], [sine, cosine]])
    both = np.stack([ahead, behind]).astype(np.float32)
    high = both.astype(jnp.bfloat16)
    low = (both - high.astype(np.float32)).astype(jnp.bfloat16)
    return jnp.asarray(np.stack([high, low], axis=1))


def split(value):
    high = value.astype(bf16)
    low = (value - high.astype(f32)).astype(bf16)
    return high, low


def dot(a, b):
    return jnp.dot(a, b, preferred_element_type=f32)


def table_left(table, value):
    high, low = split(value)
    return dot(table[0], high) + dot(table[0], low) + dot(table[1], high)


def table_right(value, table):
    high, low = split(value)
    return dot(high, table[0]) + dot(low, table[0]) + dot(high, table[1])


def gradient_kernel(starts, own, following, measured, probe, tables, spread):
    side = own.shape[1]
    count = measured.shape[0]
    ahead = (tables[0, 0], tables[0, 1])
    behind = (tables[1, 0], tables[1, 1])
    wide_real = jnp.concatenate([own[0], following[0]], axis=1)
    wide_imag = jnp.concatenate([own[1], following[1]], axis=1)
    probe_real = probe[0]
    probe_imag = probe[1]
    exits = []
    for p in range(count):
        by = lax.rem(2 * side - starts[p], 2 * side)
        patch_real = pltpu.roll(wide_real, by, 1)[:, :side]
        patch_imag = pltpu.roll(wide_imag, by, 1)[:, :side]
        exit_real = probe_real * patch_real - probe_imag * patch_imag
        exit_imag = probe_real * patch_imag + probe_imag * patch_real
        exits.append(jnp.concatenate([exit_real, exit_imag], axis=0))
    exitw = jnp.concatenate(exits, axis=1)
    left = table_left(ahead, exitw)

    def to_rows(value):
        return jnp.concatenate(
            [
                jnp.concatenate(
                    [
                        value[:side, p * side : (p + 1) * side],
                        value[side:, p * side : (p + 1) * side],
                    ],
                    axis=1,
                )
                for p in range(count)
            ],
            axis=0,
        )

    def to_columns(value):
        return jnp.concatenate(
            [
                jnp.concatenate(
                    [
                        value[p * side : (p + 1) * side, :side],
                        value[p * side : (p + 1) * side, side:],
                    ],
                    axis=0,
                )
                for p in range(count)
            ],
            axis=1,
        )

    far = table_right(to_rows(left), behind)
    far_real = far[:, :side]
    far_imag = far[:, side:]
    level = jnp.concatenate([measured[p] for p in range(count)], axis=0)
    factor = level * lax.rsqrt(far_real * far_real + far_imag * far_imag + 1.0)
    fixed = jnp.concatenate([far_real * factor, far_imag * factor], axis=1)
    back = table_left(behind, to_columns(table_right(fixed, ahead)))
    delta = back - exitw
    total_real = jnp.zeros((side, 2 * side), f32)
    total_imag = jnp.zeros((side, 2 * side), f32)
    nothing = jnp.zeros((side, side), f32)
    for p in range(count):
        delta_real = delta[:side, p * side : (p + 1) * side]
        delta_imag = delta[side:, p * side : (p + 1) * side]
        grad_real = probe_real * delta_real + probe_imag * delta_imag
        grad_imag = probe_real * delta_imag - probe_imag * delta_real
        total_real += pltpu.roll(jnp.concatenate([grad_real, nothing], axis=1), starts[p], 1)
        total_imag += pltpu.roll(jnp.concatenate([grad_imag, nothing], axis=1), starts[p], 1)
    spread[0, 0] = total_real[:, :side]
    spread[0, 1] = total_imag[:, :side]
    spread[1, 0] = total_real[:, side:]
    spread[1, 1] = total_imag[:, side:]


def gradient(starts, own, following, measured, probe, tables):
    vmem = pl.BlockSpec(memory_space=pltpu.VMEM)
    return pl.pallas_call(
        gradient_kernel,
        out_shape=jax.ShapeDtypeStruct((2,) + own.shape, f32),
        in_specs=[pl.BlockSpec(memory_space=pltpu.SMEM)] + [vmem] * 5,
        out_specs=vmem,
        compiler_params=pltpu.CompilerParams(vmem_limit_bytes=32 * 1024 * 1024),
    )(starts, own, following, measured, probe, tables)


def shear_kernel(scale, lines, into, source, choice, out, plain, taps, result):
    channels = choice.shape[0]
    side = source.shape[1]
    pieces = source.shape[0] // (lines * channels)
    span = into * side
    plain[...] = source[...].astype(f32)
    for r in range(lines):
        near = plain[pl.ds(r, channels, stride=pieces * lines), :]
        if pieces == 1:
            edge = jnp.zeros_like(near)
        else:
            edge = plain[pl.ds(lines + r, channels, stride=pieces * lines), :]
        wide = jnp.concatenate([near, edge], axis=1)
        for d in range(TAPS):
            moved = pltpu.roll(wide, (2 * side + HALO - d) % (2 * side), 1)[:, :span]
            taps[d * channels : (d + 1) * channels, r * span : (r + 1) * span] = moved.astype(bf16)
    summed = dot(choice[...], taps[...]) * scale
    for r in range(lines):
        for j in range(into):
            begin = r * span + j * side
            result[pl.ds(j * lines + r, channels, stride=into * lines), :] = summed[
                :, begin : begin + side
            ]
    out[...] = result[...].astype(bf16)


def shear_sum(source, choice, scale, lines, into):
    channels = choice.shape[0]
    side = source.shape[1]
    pieces = source.shape[0] // (lines * channels)
    vmem = pl.BlockSpec(memory_space=pltpu.VMEM)
    return pl.pallas_call(
        lambda *refs: shear_kernel(scale, lines, into, *refs),
        out_shape=jax.ShapeDtypeStruct((into * lines * channels, side), bf16),
        in_specs=[vmem] * 2,
        out_specs=vmem,
        scratch_shapes=[
            pltpu.VMEM((pieces * lines * channels, side), f32),
            pltpu.VMEM((TAPS * channels, into * lines * side), bf16),
            pltpu.VMEM((into * lines * channels, side), f32),
        ],
        compiler_params=pltpu.CompilerParams(vmem_limit_bytes=32 * 1024 * 1024),
    )(source, choice)


def strip_move(value, by):
    length = lax.axis_size("strip")
    pairs = [(i, i + by) for i in range(length) if 0 <= i + by < length]
    return lax.ppermute(value, "strip", pairs)


def with_edges(value, before, after):
    lane = lax.broadcasted_iota(jnp.int32, value.shape, value.ndim - 1)
    return jnp.where(lane < value.shape[-1] // 2, after, before)


def exchange(parts, groups):
    side = parts[0].shape[-1]
    lines = parts[0].size // (groups * side)
    parcel = jnp.concatenate([part.reshape(groups, lines, side) for part in parts], axis=1)
    got = lax.all_to_all(parcel, "view", 0, 0, tiled=True)
    return got.reshape(groups * len(parts) * lines, side)


def give_back(value, groups):
    side = value.shape[-1]
    parcel = value.reshape(groups, value.shape[0] // groups, side)
    return lax.all_to_all(parcel, "view", 0, 0, tiled=True)


def per_device(slab, psi_start, dual, amplitudes, offsets, angles, probe):
    slices = lax.axis_size("view")
    own_slab = slab[0]
    shape = own_slab.shape
    psi = psi_start[0]
    own_dual = dual[0]
    measured = amplitudes[0]
    starts = offsets[0]
    root_scale = 1.0 / math.sqrt(slices)
    tables = dft_blocks(probe.shape[1])
    step_size = 1.0 / starts.shape[0]

    depth = jnp.arange(slices, dtype=jnp.int32)
    tilt = angles - HALO
    shift = (tilt[:, None] * (2 * depth[None, :] - slices + 1)) // slices
    tap = jnp.arange(TAPS, dtype=jnp.int32) - HALO
    choice_project = (
        (shift[:, None, :] == tap[None, :, None]).astype(bf16).reshape(slices, TAPS * slices)
    )
    choice_back = (
        (-shift.T[:, None, :] == tap[None, :, None]).astype(bf16).reshape(slices, TAPS * slices)
    )

    lines = shape[0] * shape[1] // slices
    last = lax.axis_index("strip") == lax.axis_size("strip") - 1
    first = lax.axis_index("strip") == 0
    following = strip_move(psi, -1)
    lined = exchange([own_slab], slices)
    sums = shear_sum(lined, choice_project, root_scale, lines, 2)
    sums, following = lax.optimization_barrier((sums, following))
    sums = give_back(sums, slices)
    spread = gradient(starts, psi, following, measured, probe, tables)
    projected = sums[:, :lines].reshape(shape).astype(f32)
    beyond = sums[:, lines:].reshape(shape)
    pull = projected - own_dual
    psi = psi + step_size * spread[0] + coupling * (pull - psi)
    outer = step_size * spread[1]

    beyond_two = strip_move(beyond, -2)
    up = strip_move(jnp.stack([outer.astype(bf16), beyond]), 1)
    down = strip_move(jnp.stack([psi.astype(bf16), beyond]), -1)
    gain = with_edges(beyond, down[1], up[1]).astype(f32)
    pull = pull + gain
    psi = psi + up[0].astype(f32) + coupling * gain
    gain = with_edges(beyond, beyond_two, beyond).astype(f32)
    following = jnp.where(last, 0.0, down[0].astype(f32) + outer + coupling * gain)
    spread = gradient(starts, psi, following, measured, probe, tables)
    part = psi + step_size * spread[0] + coupling * (pull - psi)
    rest = (pull - part).astype(bf16)
    outer = (spread[1] * step_size).astype(bf16)
    up = strip_move(jnp.stack([rest, outer]), 1)
    up_two = strip_move(outer, 2)
    down = strip_move(rest, -1)
    incoming = up[1].astype(f32)
    psi = part + incoming
    residual = (pull - psi).astype(bf16)
    residual_edge = with_edges(
        residual,
        (up[0].astype(f32) - up_two.astype(f32)).astype(bf16),
        (down.astype(f32) - outer.astype(f32)).astype(bf16),
    )
    lane = lax.broadcasted_iota(jnp.int32, shape, 2)
    outside = (last & (lane < shape[2] // 2)) | (first & (lane >= shape[2] // 2))
    residual_edge = jnp.where(outside, jnp.zeros_like(residual_edge), residual_edge)
    lined = exchange([residual, residual_edge], slices)
    sums = shear_sum(lined, choice_back, descent * root_scale, lines, 1)
    backward = give_back(sums, slices).reshape(shape).astype(f32)
    slab_new = (own_slab.astype(f32) - backward).astype(bf16)
    return (psi[None], slab_new[None])


def solution(mesh):
    return jax.shard_map(
        per_device,
        mesh=mesh,
        in_specs=(
            P("view", None, None, "strip"),
            P("view", None, None, "strip"),
            P("view", None, None, "strip"),
            P("view", "strip", None, None),
            P("view", "strip"),
            P(),
            P(),
        ),
        out_specs=(P("view", None, None, "strip"), P("view", None, None, "strip")),
        check_vma=False,
    )
```

```python
import math

import jax
import jax.numpy as jnp
import numpy as np
from jax import lax
from jax.experimental import pallas as pl
from jax.experimental.pallas import tpu as pltpu
from jax.sharding import PartitionSpec as P

HALO = 16
ITERS = 2
TAPS = 2 * HALO + 1
coupling = 0.5
descent = 0.5
bf16 = jnp.bfloat16
f32 = jnp.float32


def dft_blocks(length):
    counter = np.arange(length)
    phase = (counter[:, None] * counter[None, :]) % length
    angle = phase.astype(np.float64) * (2.0 * math.pi / length)
    cosine = np.cos(angle) / math.sqrt(length)
    sine = np.sin(angle) / math.sqrt(length)
    ahead = np.block([[cosine, sine], [-sine, cosine]])
    behind = np.block([[cosine, -sine], [sine, cosine]])
    both = np.stack([ahead, behind]).astype(np.float32)
    high = both.astype(jnp.bfloat16)
    low = (both - high.astype(np.float32)).astype(jnp.bfloat16)
    return jnp.asarray(np.stack([high, low], axis=1))


def split(value):
    high = value.astype(bf16)
    low = (value - high.astype(f32)).astype(bf16)
    return high, low


def dot(a, b):
    return jnp.dot(a, b, preferred_element_type=f32)


def table_left(table, value):
    high, low = split(value)
    return dot(table[0], high) + dot(table[0], low) + dot(table[1], high)


def table_right(value, table):
    high, low = split(value)
    return dot(high, table[0]) + dot(low, table[0]) + dot(high, table[1])


def gradient_sums(starts, wide_real, wide_imag, measured, probe, tables):
    side = measured.shape[1]
    count = measured.shape[0]
    ahead = (tables[0, 0], tables[0, 1])
    behind = (tables[1, 0], tables[1, 1])
    probe_real = probe[0]
    probe_imag = probe[1]
    exits = []
    for p in range(count):
        by = lax.rem(2 * side - starts[p], 2 * side)
        patch_real = pltpu.roll(wide_real, by, 1)[:, :side]
        patch_imag = pltpu.roll(wide_imag, by, 1)[:, :side]
        exit_real = probe_real * patch_real - probe_imag * patch_imag
        exit_imag = probe_real * patch_imag + probe_imag * patch_real
        exits.append(jnp.concatenate([exit_real, exit_imag], axis=0))
    exitw = jnp.concatenate(exits, axis=1)
    left = table_left(ahead, exitw)

    def to_rows(value):
        return jnp.concatenate(
            [
                jnp.concatenate(
                    [
                        value[:side, p * side : (p + 1) * side],
                        value[side:, p * side : (p + 1) * side],
                    ],
                    axis=1,
                )
                for p in range(count)
            ],
            axis=0,
        )

    def to_columns(value):
        return jnp.concatenate(
            [
                jnp.concatenate(
                    [
                        value[p * side : (p + 1) * side, :side],
                        value[p * side : (p + 1) * side, side:],
                    ],
                    axis=0,
                )
                for p in range(count)
            ],
            axis=1,
        )

    far = table_right(to_rows(left), behind)
    far_real = far[:, :side]
    far_imag = far[:, side:]
    level = jnp.concatenate([measured[p] for p in range(count)], axis=0)
    factor = level * lax.rsqrt(far_real * far_real + far_imag * far_imag + 1.0)
    fixed = jnp.concatenate([far_real * factor, far_imag * factor], axis=1)
    back = table_left(behind, to_columns(table_right(fixed, ahead)))
    delta = back - exitw
    total_real = jnp.zeros((side, 2 * side), f32)
    total_imag = jnp.zeros((side, 2 * side), f32)
    nothing = jnp.zeros((side, side), f32)
    for p in range(count):
        delta_real = delta[:side, p * side : (p + 1) * side]
        delta_imag = delta[side:, p * side : (p + 1) * side]
        grad_real = probe_real * delta_real + probe_imag * delta_imag
        grad_imag = probe_real * delta_imag - probe_imag * delta_real
        total_real += pltpu.roll(jnp.concatenate([grad_real, nothing], axis=1), starts[p], 1)
        total_imag += pltpu.roll(jnp.concatenate([grad_imag, nothing], axis=1), starts[p], 1)
    return total_real, total_imag


def pack_edges(source, lines):
    side = source.shape[1]
    count = source.shape[0] // lines
    lane = lax.broadcasted_iota(jnp.int32, (count, side), 1)
    packed = jnp.zeros((count, side), f32)
    for r in range(lines):
        part = source[pl.ds(r, count, stride=lines), :]
        part = pltpu.roll(part, (HALO + 2 * HALO * r) % side, 1)
        packed = jnp.where(lane // (2 * HALO) == r, part, packed)
    return packed


def open_edges(packed, r):
    side = packed.shape[1]
    lane = lax.broadcasted_iota(jnp.int32, packed.shape, 1)
    part = pltpu.roll(packed, (2 * side - HALO - 2 * HALO * r) % side, 1)
    return jnp.where((lane < HALO) | (lane >= side - HALO), part, 0.0)


def first_kernel(starts, own, following, measured, probe, tables, spread):
    side = own.shape[1]
    wide_real = jnp.concatenate([own[0], following[0]], axis=1)
    wide_imag = jnp.concatenate([own[1], following[1]], axis=1)
    total_real, total_imag = gradient_sums(
        starts, wide_real, wide_imag, measured, probe, tables
    )
    share = 1.0 / measured.shape[0]
    spread[0, 0] = total_real[:, :side] * share
    spread[0, 1] = total_imag[:, :side] * share
    spread[1, 0] = total_real[:, side:] * share
    spread[1, 1] = total_imag[:, side:] * share


def first_gradient(starts, own, following, measured, probe, tables):
    vmem = pl.BlockSpec(memory_space=pltpu.VMEM)
    return pl.pallas_call(
        first_kernel,
        out_shape=jax.ShapeDtypeStruct((2,) + own.shape, f32),
        in_specs=[pl.BlockSpec(memory_space=pltpu.SMEM)] + [vmem] * 5,
        out_specs=vmem,
        compiler_params=pltpu.CompilerParams(vmem_limit_bytes=32 * 1024 * 1024),
    )(starts, own, following, measured, probe, tables)


def between_kernel(
    lines, odd, sums, spread, psi, dual, base, pull, send_pair, send_next, edges, plain, lined
):
    side = psi.shape[2]
    rows = 2 * psi.shape[1]
    groups = rows // lines
    stride = lines + 2
    plain[...] = sums[...].astype(f32)
    for r in range(lines):
        lined[pl.ds(r, groups, stride=lines), :] = plain[pl.ds(r, groups, stride=stride), :]
    edge = plain[pl.ds(lines, groups, stride=stride), :].astype(bf16)
    known = lined[...] - dual[...].reshape(rows, side)
    before = psi[...].reshape(rows, side)
    fresh = before + spread[0].reshape(rows, side) + coupling * (known - before)
    pull[...] = known
    base[...] = fresh
    outer = spread[1].reshape(rows, side)
    send_pair[:rows] = jnp.where(odd[0] > 0, fresh, outer).astype(bf16)
    send_pair[rows:] = edge
    send_next[:rows] = jnp.where(odd[0] > 0, outer, fresh).astype(bf16)
    send_next[rows:] = edge
    edges[...] = edge


def between(odd, sums, spread, psi, dual, lines):
    side = psi.shape[2]
    rows = 2 * psi.shape[1]
    groups = rows // lines
    vmem = pl.BlockSpec(memory_space=pltpu.VMEM)
    return pl.pallas_call(
        lambda *refs: between_kernel(lines, *refs),
        out_shape=[
            jax.ShapeDtypeStruct((rows, side), f32),
            jax.ShapeDtypeStruct((rows, side), f32),
            jax.ShapeDtypeStruct((rows + groups, side), bf16),
            jax.ShapeDtypeStruct((rows + groups, side), bf16),
            jax.ShapeDtypeStruct((groups, side), bf16),
        ],
        in_specs=[pl.BlockSpec(memory_space=pltpu.SMEM)] + [vmem] * 4,
        out_specs=[vmem] * 5,
        scratch_shapes=[
            pltpu.VMEM((groups * (lines + 2), side), f32),
            pltpu.VMEM((rows, side), f32),
        ],
        compiler_params=pltpu.CompilerParams(vmem_limit_bytes=32 * 1024 * 1024),
    )(odd, sums, spread, psi, dual)


def second_kernel(
    lines, starts, inside, base, pull, spread, pair, beside, edges, two, measured, probe, tables,
    part, want, send, rim, near, far,
):
    side = base.shape[1]
    rows = base.shape[0]
    high = rows // 2
    groups = rows // lines
    lane = lax.broadcasted_iota(jnp.int32, (groups, side), 1)
    early = lane < side // 2
    odd = inside[1] > 0
    up = jnp.where(odd, pair[...].astype(f32), beside[...].astype(f32))
    down = jnp.where(odd, beside[...].astype(f32), pair[...].astype(f32))
    here = edges[...].astype(f32)
    farther = two[...].astype(f32)
    for r in range(lines):
        near[pl.ds(r, groups, stride=lines), :] = jnp.where(
            early, open_edges(up[rows:], r), open_edges(down[rows:], r)
        )
        far[pl.ds(r, groups, stride=lines), :] = jnp.where(
            early, open_edges(here, r), open_edges(farther, r)
        )
    gain = near[...]
    drawn = pull[...] + gain
    psi = base[...] + up[:rows] + coupling * gain
    beyond = down[:rows] + spread[1].reshape(rows, side) + coupling * far[...]
    beyond = jnp.where(inside[0] > 0, beyond, 0.0)
    wide_real = jnp.concatenate([psi[:high], beyond[:high]], axis=1)
    wide_imag = jnp.concatenate([psi[high:], beyond[high:]], axis=1)
    total_real, total_imag = gradient_sums(
        starts, wide_real, wide_imag, measured, probe, tables
    )
    total = jnp.concatenate([total_real, total_imag], axis=0) * (1.0 / measured.shape[0])
    mine = psi + total[:, :side] + coupling * (drawn - psi)
    rest = drawn - mine
    part[...] = mine
    want[...] = drawn
    send[:rows] = total[:, side:].astype(bf16)
    near[...] = rest
    send[rows:] = pack_edges(near, lines).astype(bf16)
    far[...] = total[:, side:]
    rim[...] = pack_edges(far, lines).astype(bf16)


def second_gradient(
    starts, inside, base, pull, spread, pair, beside, edges, two, measured, probe, tables, lines
):
    rows, side = base.shape
    groups = rows // lines
    smem = pl.BlockSpec(memory_space=pltpu.SMEM)
    vmem = pl.BlockSpec(memory_space=pltpu.VMEM)
    return pl.pallas_call(
        lambda *refs: second_kernel(lines, *refs),
        out_shape=[
            jax.ShapeDtypeStruct((rows, side), f32),
            jax.ShapeDtypeStruct((rows, side), f32),
            jax.ShapeDtypeStruct((rows + groups, side), bf16),
            jax.ShapeDtypeStruct((groups, side), bf16),
        ],
        in_specs=[smem] * 2 + [vmem] * 10,
        out_specs=[vmem] * 4,
        scratch_shapes=[pltpu.VMEM((rows, side), f32), pltpu.VMEM((rows, side), f32)],
        compiler_params=pltpu.CompilerParams(vmem_limit_bytes=32 * 1024 * 1024),
    )(starts, inside, base, pull, spread, pair, beside, edges, two, measured, probe, tables)


def close_kernel(lines, ends, part, want, pair, beside, two, rim, psi, parcel, plain, lined):
    rows, side = part.shape
    groups = rows // lines
    stride = lines + 2
    odd = ends[2] > 0
    up = jnp.where(odd, pair[...].astype(f32), beside[...].astype(f32))
    down = jnp.where(odd, beside[rows:].astype(f32), pair[rows:].astype(f32))
    settled = part[...] + up[:rows]
    psi[...] = settled
    lined[...] = want[...] - settled
    for r in range(lines):
        plain[pl.ds(r, groups, stride=stride), :] = lined[pl.ds(r, groups, stride=lines), :]
    lane = lax.broadcasted_iota(jnp.int32, (groups, side), 1)
    left = jnp.where(ends[0] > 0, up[rows:] - two[...].astype(f32), 0.0)
    right = jnp.where(ends[1] > 0, down - rim[...].astype(f32), 0.0)
    packed = jnp.where(lane % (2 * HALO) < HALO, left, right)
    plain[pl.ds(lines, groups, stride=stride), :] = packed
    plain[pl.ds(lines + 1, groups, stride=stride), :] = jnp.zeros((groups, side), f32)
    parcel[...] = plain[...].astype(bf16)


def close(ends, part, want, pair, beside, two, rim, lines):
    rows, side = part.shape
    groups = rows // lines
    smem = pl.BlockSpec(memory_space=pltpu.SMEM)
    vmem = pl.BlockSpec(memory_space=pltpu.VMEM)
    return pl.pallas_call(
        lambda *refs: close_kernel(lines, *refs),
        out_shape=[
            jax.ShapeDtypeStruct((rows, side), f32),
            jax.ShapeDtypeStruct((groups * (lines + 2), side), bf16),
        ],
        in_specs=[smem] + [vmem] * 6,
        out_specs=[vmem] * 2,
        scratch_shapes=[
            pltpu.VMEM((groups * (lines + 2), side), f32),
            pltpu.VMEM((rows, side), f32),
        ],
        compiler_params=pltpu.CompilerParams(vmem_limit_bytes=32 * 1024 * 1024),
    )(ends, part, want, pair, beside, two, rim)


def shear_kernel(scale, lines, wide_out, source, choice, out, plain, taps, result):
    channels = choice.shape[0]
    side = source.shape[1]
    pieces = source.shape[0] // channels
    span = 2 * side if wide_out else side
    plain[...] = source[...].astype(f32)
    if pieces > lines:
        packed = plain[pl.ds(lines, channels, stride=pieces), :]
    for r in range(lines):
        near = plain[pl.ds(r, channels, stride=pieces), :]
        edge = open_edges(packed, r) if pieces > lines else jnp.zeros_like(near)
        wide = jnp.concatenate([near, edge], axis=1)
        for d in range(TAPS):
            moved = pltpu.roll(wide, (2 * side + HALO - d) % (2 * side), 1)[:, :span]
            taps[d * channels : (d + 1) * channels, r * span : (r + 1) * span] = moved.astype(bf16)
    summed = dot(choice[...], taps[...]) * scale
    given = lines + 2 if wide_out else lines
    for r in range(lines):
        result[pl.ds(r, channels, stride=given), :] = summed[:, r * span : r * span + side]
    if wide_out:
        lane = lax.broadcasted_iota(jnp.int32, (channels, side), 1)
        packed = jnp.zeros((channels, side), f32)
        for r in range(lines):
            part = summed[:, r * span + side : (r + 1) * span]
            part = pltpu.roll(part, (HALO + 2 * HALO * r) % side, 1)
            packed = jnp.where(lane // (2 * HALO) == r, part, packed)
        result[pl.ds(lines, channels, stride=given), :] = packed
        result[pl.ds(lines + 1, channels, stride=given), :] = jnp.zeros_like(packed)
    out[...] = result[...].astype(bf16)


def shear_sum(source, choice, scale, lines, wide_out):
    channels = choice.shape[0]
    side = source.shape[1]
    given = (lines + 2 if wide_out else lines) * channels
    span = 2 * side if wide_out else side
    vmem = pl.BlockSpec(memory_space=pltpu.VMEM)
    return pl.pallas_call(
        lambda *refs: shear_kernel(scale, lines, wide_out, *refs),
        out_shape=jax.ShapeDtypeStruct((given, side), bf16),
        in_specs=[vmem] * 2,
        out_specs=vmem,
        scratch_shapes=[
            pltpu.VMEM(source.shape, f32),
            pltpu.VMEM((TAPS * channels, lines * span), bf16),
            pltpu.VMEM((given, side), f32),
        ],
        compiler_params=pltpu.CompilerParams(vmem_limit_bytes=32 * 1024 * 1024),
    )(source, choice)


def strip_move(value, by):
    length = lax.axis_size("strip")
    pairs = [(i, i + by) for i in range(length) if 0 <= i + by < length]
    return lax.ppermute(value, "strip", pairs)


def strip_swap(value, begin):
    pairs = []
    for i in range(begin, lax.axis_size("strip") - 1, 2):
        pairs += [(i, i + 1), (i + 1, i)]
    return lax.ppermute(value, "strip", pairs)


def regroup(value, groups):
    side = value.shape[-1]
    parcel = value.reshape(groups, value.shape[0] // (2 * groups), 2, side)
    return lax.all_to_all(parcel, "view", 0, 0, tiled=True).reshape(value.shape)


def per_device(slab, psi_start, dual, amplitudes, offsets, angles, probe):
    slices = lax.axis_size("view")
    own_slab = slab[0]
    shape = own_slab.shape
    psi = psi_start[0]
    own_dual = dual[0]
    measured = amplitudes[0]
    starts = offsets[0]
    root_scale = 1.0 / math.sqrt(slices)
    tables = dft_blocks(probe.shape[1])

    depth = jnp.arange(slices, dtype=jnp.int32)
    tilt = angles - HALO
    shift = (tilt[:, None] * (2 * depth[None, :] - slices + 1)) // slices
    tap = jnp.arange(TAPS, dtype=jnp.int32) - HALO
    choice_project = (
        (shift[:, None, :] == tap[None, :, None]).astype(bf16).reshape(slices, TAPS * slices)
    )
    choice_back = (
        (-shift.T[:, None, :] == tap[None, :, None]).astype(bf16).reshape(slices, TAPS * slices)
    )

    lines = shape[0] * shape[1] // slices
    place = lax.axis_index("strip")
    odd = place % 2
    inside = (place < lax.axis_size("strip") - 1).astype(jnp.int32)
    ends = jnp.stack([(place > 0).astype(jnp.int32), inside, odd])
    following = strip_move(psi, -1)
    lined = regroup(own_slab.reshape(lines * slices, shape[2]), slices)
    sums = shear_sum(lined, choice_project, root_scale, lines, True)
    sums, following = lax.optimization_barrier((sums, following))
    sums = regroup(sums, slices)
    spread = first_gradient(starts, psi, following, measured, probe, tables)
    base, pull, pair, beside, edges = between(ends[2:], sums, spread, psi, own_dual, lines)
    two = strip_move(edges, -2)
    beside = strip_swap(beside, 1)
    pair = strip_swap(pair, 0)
    part, want, send, rim = second_gradient(
        starts, ends[1:], base, pull, spread, pair, beside, edges, two, measured, probe, tables,
        lines,
    )
    two = strip_move(rim, 2)
    beside = strip_swap(send, 1)
    pair = strip_swap(send, 0)
    psi, parcel = close(ends, part, want, pair, beside, two, rim, lines)
    psi = psi.reshape(shape)
    lined = regroup(parcel, slices)
    sums = shear_sum(lined, choice_back, descent * root_scale, lines, False)
    backward = regroup(sums, slices).reshape(shape).astype(f32)
    slab_new = (own_slab.astype(f32) - backward).astype(bf16)
    return (psi[None], slab_new[None])


def solution(mesh):
    return jax.shard_map(
        per_device,
        mesh=mesh,
        in_specs=(
            P("view", None, None, "strip"),
            P("view", None, None, "strip"),
            P("view", None, None, "strip"),
            P("view", "strip", None, None),
            P("view", "strip"),
            P(),
            P(),
        ),
        out_specs=(P("view", None, None, "strip"), P("view", None, None, "strip")),
        check_vma=False,
    )
```

```python
import math

import jax
import jax.numpy as jnp
import numpy as np
from jax import lax
from jax.experimental import pallas as pl
from jax.experimental.pallas import tpu as pltpu
from jax.sharding import PartitionSpec as P

HALO = 16
ITERS = 2
TAPS = 2 * HALO + 1
coupling = 0.5
descent = 0.5
bf16 = jnp.bfloat16
f32 = jnp.float32


def dft_blocks(length):
    counter = np.arange(length)
    phase = (counter[:, None] * counter[None, :]) % length
    angle = phase.astype(np.float64) * (2.0 * math.pi / length)
    cosine = np.cos(angle) / math.sqrt(length)
    sine = np.sin(angle) / math.sqrt(length)
    ahead = np.block([[cosine, sine], [-sine, cosine]])
    behind = np.block([[cosine, -sine], [sine, cosine]])
    both = np.stack([ahead, behind]).astype(np.float32)
    high = both.astype(jnp.bfloat16)
    low = (both - high.astype(np.float32)).astype(jnp.bfloat16)
    return jnp.asarray(np.stack([high, low], axis=1))


def split(value):
    high = value.astype(bf16)
    low = (value - high.astype(f32)).astype(bf16)
    return high, low


def dot(a, b):
    return jnp.dot(a, b, preferred_element_type=f32)


def table_left(table, value):
    high, low = split(value)
    return dot(table[0], high) + dot(table[0], low) + dot(table[1], high)


def table_right(value, table):
    high, low = split(value)
    return dot(high, table[0]) + dot(low, table[0]) + dot(high, table[1])


def gradient_sums(starts, wide_real, wide_imag, measured, probe, tables):
    side = measured.shape[1]
    count = measured.shape[0]
    ahead = (tables[0, 0], tables[0, 1])
    behind = (tables[1, 0], tables[1, 1])
    probe_real = probe[0]
    probe_imag = probe[1]
    exits = []
    for p in range(count):
        by = lax.rem(2 * side - starts[p], 2 * side)
        patch_real = pltpu.roll(wide_real, by, 1)[:, :side]
        patch_imag = pltpu.roll(wide_imag, by, 1)[:, :side]
        exit_real = probe_real * patch_real - probe_imag * patch_imag
        exit_imag = probe_real * patch_imag + probe_imag * patch_real
        exits.append(jnp.concatenate([exit_real, exit_imag], axis=0))
    exitw = jnp.concatenate(exits, axis=1)
    left = table_left(ahead, exitw)

    def to_rows(value):
        return jnp.concatenate(
            [
                jnp.concatenate(
                    [
                        value[:side, p * side : (p + 1) * side],
                        value[side:, p * side : (p + 1) * side],
                    ],
                    axis=1,
                )
                for p in range(count)
            ],
            axis=0,
        )

    def to_columns(value):
        return jnp.concatenate(
            [
                jnp.concatenate(
                    [
                        value[p * side : (p + 1) * side, :side],
                        value[p * side : (p + 1) * side, side:],
                    ],
                    axis=0,
                )
                for p in range(count)
            ],
            axis=1,
        )

    far = table_right(to_rows(left), behind)
    far_real = far[:, :side]
    far_imag = far[:, side:]
    level = jnp.concatenate([measured[p] for p in range(count)], axis=0)
    factor = level * lax.rsqrt(far_real * far_real + far_imag * far_imag + 1.0)
    fixed = jnp.concatenate([far_real * factor, far_imag * factor], axis=1)
    back = table_left(behind, to_columns(table_right(fixed, ahead)))
    delta = back - exitw
    total_real = jnp.zeros((side, 2 * side), f32)
    total_imag = jnp.zeros((side, 2 * side), f32)
    nothing = jnp.zeros((side, side), f32)
    for p in range(count):
        delta_real = delta[:side, p * side : (p + 1) * side]
        delta_imag = delta[side:, p * side : (p + 1) * side]
        grad_real = probe_real * delta_real + probe_imag * delta_imag
        grad_imag = probe_real * delta_imag - probe_imag * delta_real
        total_real += pltpu.roll(jnp.concatenate([grad_real, nothing], axis=1), starts[p], 1)
        total_imag += pltpu.roll(jnp.concatenate([grad_imag, nothing], axis=1), starts[p], 1)
    return total_real, total_imag


def pack_edges(source, lines):
    side = source.shape[1]
    count = source.shape[0] // lines
    lane = lax.broadcasted_iota(jnp.int32, (count, side), 1)
    packed = jnp.zeros((count, side), f32)
    for r in range(lines):
        part = source[pl.ds(r, count, stride=lines), :]
        part = pltpu.roll(part, (HALO + 2 * HALO * r) % side, 1)
        packed = jnp.where(lane // (2 * HALO) == r, part, packed)
    return packed


def open_edges(packed, r):
    side = packed.shape[1]
    lane = lax.broadcasted_iota(jnp.int32, packed.shape, 1)
    part = pltpu.roll(packed, (2 * side - HALO - 2 * HALO * r) % side, 1)
    return jnp.where((lane < HALO) | (lane >= side - HALO), part, 0.0)


def first_kernel(starts, own, following, measured, probe, tables, spread):
    side = own.shape[1]
    wide_real = jnp.concatenate([own[0], following[0]], axis=1)
    wide_imag = jnp.concatenate([own[1], following[1]], axis=1)
    total_real, total_imag = gradient_sums(
        starts, wide_real, wide_imag, measured, probe, tables
    )
    share = 1.0 / measured.shape[0]
    spread[0, 0] = total_real[:, :side] * share
    spread[0, 1] = total_imag[:, :side] * share
    spread[1, 0] = total_real[:, side:] * share
    spread[1, 1] = total_imag[:, side:] * share


def first_gradient(starts, own, following, measured, probe, tables):
    vmem = pl.BlockSpec(memory_space=pltpu.VMEM)
    return pl.pallas_call(
        first_kernel,
        out_shape=jax.ShapeDtypeStruct((2,) + own.shape, f32),
        in_specs=[pl.BlockSpec(memory_space=pltpu.SMEM)] + [vmem] * 5,
        out_specs=vmem,
        compiler_params=pltpu.CompilerParams(vmem_limit_bytes=32 * 1024 * 1024),
    )(starts, own, following, measured, probe, tables)


def between_kernel(
    lines, odd, sums, spread, psi, dual, base, pull, send_pair, send_next, edges, plain, lined
):
    side = psi.shape[2]
    rows = 2 * psi.shape[1]
    groups = rows // lines
    stride = lines + 2
    plain[...] = sums[...].astype(f32)
    for r in range(lines):
        lined[pl.ds(r, groups, stride=lines), :] = plain[pl.ds(r, groups, stride=stride), :]
    edge = plain[pl.ds(lines, groups, stride=stride), :].astype(bf16)
    known = lined[...] - dual[...].reshape(rows, side)
    before = psi[...].reshape(rows, side)
    fresh = before + spread[0].reshape(rows, side) + coupling * (known - before)
    pull[...] = known
    base[...] = fresh
    outer = spread[1].reshape(rows, side)
    send_pair[:rows] = jnp.where(odd[0] > 0, fresh, outer).astype(bf16)
    send_pair[rows:] = edge
    send_next[:rows] = jnp.where(odd[0] > 0, outer, fresh).astype(bf16)
    send_next[rows:] = edge
    edges[...] = edge


def between(odd, sums, spread, psi, dual, lines):
    side = psi.shape[2]
    rows = 2 * psi.shape[1]
    groups = rows // lines
    vmem = pl.BlockSpec(memory_space=pltpu.VMEM)
    return pl.pallas_call(
        lambda *refs: between_kernel(lines, *refs),
        out_shape=[
            jax.ShapeDtypeStruct((rows, side), f32),
            jax.ShapeDtypeStruct((rows, side), f32),
            jax.ShapeDtypeStruct((rows + groups, side), bf16),
            jax.ShapeDtypeStruct((rows + groups, side), bf16),
            jax.ShapeDtypeStruct((groups, side), bf16),
        ],
        in_specs=[pl.BlockSpec(memory_space=pltpu.SMEM)] + [vmem] * 4,
        out_specs=[vmem] * 5,
        scratch_shapes=[
            pltpu.VMEM((groups * (lines + 2), side), f32),
            pltpu.VMEM((rows, side), f32),
        ],
        compiler_params=pltpu.CompilerParams(vmem_limit_bytes=32 * 1024 * 1024),
    )(odd, sums, spread, psi, dual)


def second_kernel(
    lines, starts, inside, base, pull, spread, pair, beside, edges, two, measured, probe, tables,
    part, want, send, rim, near, far,
):
    side = base.shape[1]
    rows = base.shape[0]
    high = rows // 2
    groups = rows // lines
    lane = lax.broadcasted_iota(jnp.int32, (groups, side), 1)
    early = lane < side // 2
    odd = inside[1] > 0
    up = jnp.where(odd, pair[...].astype(f32), beside[...].astype(f32))
    down = jnp.where(odd, beside[...].astype(f32), pair[...].astype(f32))
    here = edges[...].astype(f32)
    farther = two[...].astype(f32)
    for r in range(lines):
        near[pl.ds(r, groups, stride=lines), :] = jnp.where(
            early, open_edges(up[rows:], r), open_edges(down[rows:], r)
        )
        far[pl.ds(r, groups, stride=lines), :] = jnp.where(
            early, open_edges(here, r), open_edges(farther, r)
        )
    gain = near[...]
    drawn = pull[...] + gain
    psi = base[...] + up[:rows] + coupling * gain
    beyond = down[:rows] + spread[1].reshape(rows, side) + coupling * far[...]
    beyond = jnp.where(inside[0] > 0, beyond, 0.0)
    wide_real = jnp.concatenate([psi[:high], beyond[:high]], axis=1)
    wide_imag = jnp.concatenate([psi[high:], beyond[high:]], axis=1)
    total_real, total_imag = gradient_sums(
        starts, wide_real, wide_imag, measured, probe, tables
    )
    total = jnp.concatenate([total_real, total_imag], axis=0) * (1.0 / measured.shape[0])
    mine = psi + total[:, :side] + coupling * (drawn - psi)
    rest = drawn - mine
    part[...] = mine
    want[...] = drawn
    send[:rows] = total[:, side:].astype(bf16)
    near[...] = rest
    send[rows:] = pack_edges(near, lines).astype(bf16)
    far[...] = total[:, side:]
    rim[...] = pack_edges(far, lines).astype(bf16)


def second_gradient(
    starts, inside, base, pull, spread, pair, beside, edges, two, measured, probe, tables, lines
):
    rows, side = base.shape
    groups = rows // lines
    smem = pl.BlockSpec(memory_space=pltpu.SMEM)
    vmem = pl.BlockSpec(memory_space=pltpu.VMEM)
    return pl.pallas_call(
        lambda *refs: second_kernel(lines, *refs),
        out_shape=[
            jax.ShapeDtypeStruct((rows, side), f32),
            jax.ShapeDtypeStruct((rows, side), f32),
            jax.ShapeDtypeStruct((rows + groups, side), bf16),
            jax.ShapeDtypeStruct((groups, side), bf16),
        ],
        in_specs=[smem] * 2 + [vmem] * 10,
        out_specs=[vmem] * 4,
        scratch_shapes=[pltpu.VMEM((rows, side), f32), pltpu.VMEM((rows, side), f32)],
        compiler_params=pltpu.CompilerParams(vmem_limit_bytes=32 * 1024 * 1024),
    )(starts, inside, base, pull, spread, pair, beside, edges, two, measured, probe, tables)


def close_kernel(lines, ends, part, want, pair, beside, two, rim, psi, parcel, plain, lined):
    rows, side = part.shape
    groups = rows // lines
    stride = lines + 2
    odd = ends[2] > 0
    up = jnp.where(odd, pair[...].astype(f32), beside[...].astype(f32))
    down = jnp.where(odd, beside[rows:].astype(f32), pair[rows:].astype(f32))
    settled = part[...] + up[:rows]
    psi[...] = settled
    lined[...] = want[...] - settled
    for r in range(lines):
        plain[pl.ds(r, groups, stride=stride), :] = lined[pl.ds(r, groups, stride=lines), :]
    lane = lax.broadcasted_iota(jnp.int32, (groups, side), 1)
    left = jnp.where(ends[0] > 0, up[rows:] - two[...].astype(f32), 0.0)
    right = jnp.where(ends[1] > 0, down - rim[...].astype(f32), 0.0)
    packed = jnp.where(lane % (2 * HALO) < HALO, left, right)
    plain[pl.ds(lines, groups, stride=stride), :] = packed
    plain[pl.ds(lines + 1, groups, stride=stride), :] = jnp.zeros((groups, side), f32)
    parcel[...] = plain[...].astype(bf16)


def close(ends, part, want, pair, beside, two, rim, lines):
    rows, side = part.shape
    groups = rows // lines
    smem = pl.BlockSpec(memory_space=pltpu.SMEM)
    vmem = pl.BlockSpec(memory_space=pltpu.VMEM)
    return pl.pallas_call(
        lambda *refs: close_kernel(lines, *refs),
        out_shape=[
            jax.ShapeDtypeStruct((rows, side), f32),
            jax.ShapeDtypeStruct((groups * (lines + 2), side), bf16),
        ],
        in_specs=[smem] + [vmem] * 6,
        out_specs=[vmem] * 2,
        scratch_shapes=[
            pltpu.VMEM((groups * (lines + 2), side), f32),
            pltpu.VMEM((rows, side), f32),
        ],
        compiler_params=pltpu.CompilerParams(vmem_limit_bytes=32 * 1024 * 1024),
    )(ends, part, want, pair, beside, two, rim)


def shear_kernel(scale, lines, wide_out, source, choice, out, plain, taps, result):
    channels = choice.shape[0]
    side = source.shape[1]
    pieces = source.shape[0] // channels
    span = 2 * side if wide_out else side
    plain[...] = source[...].astype(f32)
    if pieces > lines:
        packed = plain[pl.ds(lines, channels, stride=pieces), :]
    for r in range(lines):
        near = plain[pl.ds(r, channels, stride=pieces), :]
        edge = open_edges(packed, r) if pieces > lines else jnp.zeros_like(near)
        wide = jnp.concatenate([near, edge], axis=1).astype(bf16)
        for d in range(TAPS):
            moved = pltpu.roll(wide, (2 * side + HALO - d) % (2 * side), 1)[:, :span]
            taps[d * channels : (d + 1) * channels, r * span : (r + 1) * span] = moved
    summed = dot(choice[...], taps[...]) * scale
    given = lines + 2 if wide_out else lines
    for r in range(lines):
        result[pl.ds(r, channels, stride=given), :] = summed[:, r * span : r * span + side]
    if wide_out:
        lane = lax.broadcasted_iota(jnp.int32, (channels, side), 1)
        packed = jnp.zeros((channels, side), f32)
        for r in range(lines):
            part = summed[:, r * span + side : (r + 1) * span]
            part = pltpu.roll(part, (HALO + 2 * HALO * r) % side, 1)
            packed = jnp.where(lane // (2 * HALO) == r, part, packed)
        result[pl.ds(lines, channels, stride=given), :] = packed
        result[pl.ds(lines + 1, channels, stride=given), :] = jnp.zeros_like(packed)
    out[...] = result[...].astype(bf16)


def shear_sum(source, choice, scale, lines, wide_out):
    channels = choice.shape[0]
    side = source.shape[1]
    given = (lines + 2 if wide_out else lines) * channels
    span = 2 * side if wide_out else side
    vmem = pl.BlockSpec(memory_space=pltpu.VMEM)
    return pl.pallas_call(
        lambda *refs: shear_kernel(scale, lines, wide_out, *refs),
        out_shape=jax.ShapeDtypeStruct((given, side), bf16),
        in_specs=[vmem] * 2,
        out_specs=vmem,
        scratch_shapes=[
            pltpu.VMEM(source.shape, f32),
            pltpu.VMEM((TAPS * channels, lines * span), bf16),
            pltpu.VMEM((given, side), f32),
        ],
        compiler_params=pltpu.CompilerParams(vmem_limit_bytes=32 * 1024 * 1024),
    )(source, choice)


def back_kernel(scale, lines, source, choice, settled, out, psi, plain, taps, result, done):
    copy = pltpu.make_async_copy(settled, psi, done)
    copy.start()
    shear_kernel(scale, lines, False, source, choice, out, plain, taps, result)
    copy.wait()


def back_sum(source, choice, settled, scale, lines):
    channels = choice.shape[0]
    side = source.shape[1]
    vmem = pl.BlockSpec(memory_space=pltpu.VMEM)
    return pl.pallas_call(
        lambda *refs: back_kernel(scale, lines, *refs),
        out_shape=[
            jax.ShapeDtypeStruct((lines * channels, side), bf16),
            jax.ShapeDtypeStruct(settled.shape, f32),
        ],
        in_specs=[vmem] * 3,
        out_specs=[vmem, pl.BlockSpec(memory_space=pl.ANY)],
        scratch_shapes=[
            pltpu.VMEM(source.shape, f32),
            pltpu.VMEM((TAPS * channels, lines * side), bf16),
            pltpu.VMEM((lines * channels, side), f32),
            pltpu.SemaphoreType.DMA,
        ],
        compiler_params=pltpu.CompilerParams(vmem_limit_bytes=32 * 1024 * 1024),
    )(source, choice, settled)


def strip_move(value, by):
    length = lax.axis_size("strip")
    pairs = [(i, i + by) for i in range(length) if 0 <= i + by < length]
    return lax.ppermute(value, "strip", pairs)


def strip_swap(value, begin):
    pairs = []
    for i in range(begin, lax.axis_size("strip") - 1, 2):
        pairs += [(i, i + 1), (i + 1, i)]
    return lax.ppermute(value, "strip", pairs)


def regroup(value, groups):
    side = value.shape[-1]
    parcel = value.reshape(groups, value.shape[0] // (2 * groups), 2, side)
    return lax.all_to_all(parcel, "view", 0, 0, tiled=True).reshape(value.shape)


def per_device(slab, psi_start, dual, amplitudes, offsets, angles, probe):
    slices = lax.axis_size("view")
    own_slab = slab[0]
    shape = own_slab.shape
    psi = psi_start[0]
    own_dual = dual[0]
    measured = amplitudes[0]
    starts = offsets[0]
    root_scale = 1.0 / math.sqrt(slices)
    tables = dft_blocks(probe.shape[1])

    depth = jnp.arange(slices, dtype=jnp.int32)
    tilt = angles - HALO
    shift = (tilt[:, None] * (2 * depth[None, :] - slices + 1)) // slices
    tap = jnp.arange(TAPS, dtype=jnp.int32) - HALO
    choice_project = (
        (shift[:, None, :] == tap[None, :, None]).astype(bf16).reshape(slices, TAPS * slices)
    )
    choice_back = (
        (-shift.T[:, None, :] == tap[None, :, None]).astype(bf16).reshape(slices, TAPS * slices)
    )

    lines = shape[0] * shape[1] // slices
    place = lax.axis_index("strip")
    odd = place % 2
    inside = (place < lax.axis_size("strip") - 1).astype(jnp.int32)
    ends = jnp.stack([(place > 0).astype(jnp.int32), inside, odd])
    following = strip_move(psi, -1)
    lined = regroup(own_slab.reshape(lines * slices, shape[2]), slices)
    sums = shear_sum(lined, choice_project, root_scale, lines, True)
    sums, following = lax.optimization_barrier((sums, following))
    sums = regroup(sums, slices)
    spread = first_gradient(starts, psi, following, measured, probe, tables)
    base, pull, pair, beside, edges = between(ends[2:], sums, spread, psi, own_dual, lines)
    two = strip_move(edges, -2)
    beside = strip_swap(beside, 1)
    pair = strip_swap(pair, 0)
    part, want, send, rim = second_gradient(
        starts, ends[1:], base, pull, spread, pair, beside, edges, two, measured, probe, tables,
        lines,
    )
    two = strip_move(rim, 2)
    beside = strip_swap(send, 1)
    pair = strip_swap(send, 0)
    psi, parcel = close(ends, part, want, pair, beside, two, rim, lines)
    lined = regroup(parcel, slices)
    sums, psi = back_sum(lined, choice_back, psi, descent * root_scale, lines)
    psi = psi.reshape(shape)
    backward = regroup(sums, slices).reshape(shape).astype(f32)
    slab_new = (own_slab.astype(f32) - backward).astype(bf16)
    return (psi[None], slab_new[None])


def solution(mesh):
    return jax.shard_map(
        per_device,
        mesh=mesh,
        in_specs=(
            P("view", None, None, "strip"),
            P("view", None, None, "strip"),
            P("view", None, None, "strip"),
            P("view", "strip", None, None),
            P("view", "strip"),
            P(),
            P(),
        ),
        out_specs=(P("view", None, None, "strip"), P("view", None, None, "strip")),
        check_vma=False,
    )
```

```python
import math

import jax
import jax.numpy as jnp
import numpy as np
from jax import lax
from jax.experimental import pallas as pl
from jax.experimental.pallas import tpu as pltpu
from jax.sharding import PartitionSpec as P

HALO = 16
ITERS = 2
TAPS = 2 * HALO + 1
coupling = 0.5
descent = 0.5
bf16 = jnp.bfloat16
f32 = jnp.float32


def dft_blocks(length):
    counter = np.arange(length)
    phase = (counter[:, None] * counter[None, :]) % length
    angle = phase.astype(np.float64) * (2.0 * math.pi / length)
    cosine = np.cos(angle) / math.sqrt(length)
    sine = np.sin(angle) / math.sqrt(length)
    ahead = np.block([[cosine, sine], [-sine, cosine]])
    behind = np.block([[cosine, -sine], [sine, cosine]])
    both = np.stack([ahead, behind]).astype(np.float32)
    high = both.astype(jnp.bfloat16)
    low = (both - high.astype(np.float32)).astype(jnp.bfloat16)
    return jnp.asarray(np.stack([high, low], axis=1))


def split(value):
    high = value.astype(bf16)
    low = (value - high.astype(f32)).astype(bf16)
    return high, low


def dot(a, b):
    return jnp.dot(a, b, preferred_element_type=f32)


def table_left(table, value):
    high, low = split(value)
    across = jnp.concatenate([table[0], table[0], table[1]], axis=1)
    return dot(across, jnp.concatenate([high, low, high], axis=0))


def table_right(value, table):
    high, low = split(value)
    along = jnp.concatenate([table[0], table[0], table[1]], axis=0)
    return dot(jnp.concatenate([high, low, high], axis=1), along)


def gradient_sums(starts, wide_real, wide_imag, measured, probe, tables):
    side = measured.shape[1]
    count = measured.shape[0]
    ahead = (tables[0, 0], tables[0, 1])
    behind = (tables[1, 0], tables[1, 1])
    probe_real = probe[0]
    probe_imag = probe[1]
    exits = []
    for p in range(count):
        by = lax.rem(2 * side - starts[p], 2 * side)
        patch_real = pltpu.roll(wide_real, by, 1)[:, :side]
        patch_imag = pltpu.roll(wide_imag, by, 1)[:, :side]
        exit_real = probe_real * patch_real - probe_imag * patch_imag
        exit_imag = probe_real * patch_imag + probe_imag * patch_real
        exits.append(jnp.concatenate([exit_real, exit_imag], axis=0))
    exitw = jnp.concatenate(exits, axis=1)
    left = table_left(ahead, exitw)

    def to_rows(value):
        return jnp.concatenate(
            [
                jnp.concatenate(
                    [
                        value[:side, p * side : (p + 1) * side],
                        value[side:, p * side : (p + 1) * side],
                    ],
                    axis=1,
                )
                for p in range(count)
            ],
            axis=0,
        )

    def to_columns(value):
        return jnp.concatenate(
            [
                jnp.concatenate(
                    [
                        value[p * side : (p + 1) * side, :side],
                        value[p * side : (p + 1) * side, side:],
                    ],
                    axis=0,
                )
                for p in range(count)
            ],
            axis=1,
        )

    far = table_right(to_rows(left), behind)
    far_real = far[:, :side]
    far_imag = far[:, side:]
    level = jnp.concatenate([measured[p] for p in range(count)], axis=0)
    factor = level * lax.rsqrt(far_real * far_real + far_imag * far_imag + 1.0)
    fixed = jnp.concatenate([far_real * factor, far_imag * factor], axis=1)
    back = table_left(behind, to_columns(table_right(fixed, ahead)))
    delta = back - exitw
    total_real = jnp.zeros((side, 2 * side), f32)
    total_imag = jnp.zeros((side, 2 * side), f32)
    nothing = jnp.zeros((side, side), f32)
    for p in range(count):
        delta_real = delta[:side, p * side : (p + 1) * side]
        delta_imag = delta[side:, p * side : (p + 1) * side]
        grad_real = probe_real * delta_real + probe_imag * delta_imag
        grad_imag = probe_real * delta_imag - probe_imag * delta_real
        total_real += pltpu.roll(jnp.concatenate([grad_real, nothing], axis=1), starts[p], 1)
        total_imag += pltpu.roll(jnp.concatenate([grad_imag, nothing], axis=1), starts[p], 1)
    return total_real, total_imag


def pack_edges(source, lines):
    side = source.shape[1]
    count = source.shape[0] // lines
    lane = lax.broadcasted_iota(jnp.int32, (count, side), 1)
    packed = jnp.zeros((count, side), f32)
    for r in range(lines):
        part = source[pl.ds(r, count, stride=lines), :]
        part = pltpu.roll(part, (HALO + 2 * HALO * r) % side, 1)
        packed = jnp.where(lane // (2 * HALO) == r, part, packed)
    return packed


def open_edges(packed, r):
    side = packed.shape[1]
    lane = lax.broadcasted_iota(jnp.int32, packed.shape, 1)
    part = pltpu.roll(packed, (2 * side - HALO - 2 * HALO * r) % side, 1)
    return jnp.where((lane < HALO) | (lane >= side - HALO), part, 0.0)


def first_kernel(starts, own, following, measured, probe, tables, spread):
    side = own.shape[1]
    wide_real = jnp.concatenate([own[0], following[0]], axis=1)
    wide_imag = jnp.concatenate([own[1], following[1]], axis=1)
    total_real, total_imag = gradient_sums(
        starts, wide_real, wide_imag, measured, probe, tables
    )
    share = 1.0 / measured.shape[0]
    spread[0, 0] = total_real[:, :side] * share
    spread[0, 1] = total_imag[:, :side] * share
    spread[1, 0] = total_real[:, side:] * share
    spread[1, 1] = total_imag[:, side:] * share


def first_gradient(starts, own, following, measured, probe, tables):
    vmem = pl.BlockSpec(memory_space=pltpu.VMEM)
    return pl.pallas_call(
        first_kernel,
        out_shape=jax.ShapeDtypeStruct((2,) + own.shape, f32),
        in_specs=[pl.BlockSpec(memory_space=pltpu.SMEM)] + [vmem] * 5,
        out_specs=vmem,
        compiler_params=pltpu.CompilerParams(vmem_limit_bytes=32 * 1024 * 1024),
    )(starts, own, following, measured, probe, tables)


def between_kernel(
    lines, odd, sums, spread, psi, dual, base, pull, send_pair, send_next, edges, plain, lined
):
    side = psi.shape[2]
    rows = 2 * psi.shape[1]
    groups = rows // lines
    stride = lines + 2
    plain[...] = sums[...].astype(f32)
    for r in range(lines):
        lined[pl.ds(r, groups, stride=lines), :] = plain[pl.ds(r, groups, stride=stride), :]
    edge = plain[pl.ds(lines, groups, stride=stride), :].astype(bf16)
    known = lined[...] - dual[...].reshape(rows, side)
    before = psi[...].reshape(rows, side)
    fresh = before + spread[0].reshape(rows, side) + coupling * (known - before)
    pull[...] = known
    base[...] = fresh
    outer = spread[1].reshape(rows, side)
    send_pair[:rows] = jnp.where(odd[0] > 0, fresh, outer).astype(bf16)
    send_pair[rows:] = edge
    send_next[:rows] = jnp.where(odd[0] > 0, outer, fresh).astype(bf16)
    send_next[rows:] = edge
    edges[...] = edge


def between(odd, sums, spread, psi, dual, lines):
    side = psi.shape[2]
    rows = 2 * psi.shape[1]
    groups = rows // lines
    vmem = pl.BlockSpec(memory_space=pltpu.VMEM)
    return pl.pallas_call(
        lambda *refs: between_kernel(lines, *refs),
        out_shape=[
            jax.ShapeDtypeStruct((rows, side), f32),
            jax.ShapeDtypeStruct((rows, side), f32),
            jax.ShapeDtypeStruct((rows + groups, side), bf16),
            jax.ShapeDtypeStruct((rows + groups, side), bf16),
            jax.ShapeDtypeStruct((groups, side), bf16),
        ],
        in_specs=[pl.BlockSpec(memory_space=pltpu.SMEM)] + [vmem] * 4,
        out_specs=[vmem] * 5,
        scratch_shapes=[
            pltpu.VMEM((groups * (lines + 2), side), f32),
            pltpu.VMEM((rows, side), f32),
        ],
        compiler_params=pltpu.CompilerParams(vmem_limit_bytes=32 * 1024 * 1024),
    )(odd, sums, spread, psi, dual)


def second_kernel(
    lines, starts, inside, base, pull, spread, pair, beside, edges, two, measured, probe, tables,
    part, want, send, rim, near, far,
):
    side = base.shape[1]
    rows = base.shape[0]
    high = rows // 2
    groups = rows // lines
    lane = lax.broadcasted_iota(jnp.int32, (groups, side), 1)
    early = lane < side // 2
    odd = inside[1] > 0
    up = jnp.where(odd, pair[...].astype(f32), beside[...].astype(f32))
    down = jnp.where(odd, beside[...].astype(f32), pair[...].astype(f32))
    here = edges[...].astype(f32)
    farther = two[...].astype(f32)
    for r in range(lines):
        near[pl.ds(r, groups, stride=lines), :] = jnp.where(
            early, open_edges(up[rows:], r), open_edges(down[rows:], r)
        )
        far[pl.ds(r, groups, stride=lines), :] = jnp.where(
            early, open_edges(here, r), open_edges(farther, r)
        )
    gain = near[...]
    drawn = pull[...] + gain
    psi = base[...] + up[:rows] + coupling * gain
    beyond = down[:rows] + spread[1].reshape(rows, side) + coupling * far[...]
    beyond = jnp.where(inside[0] > 0, beyond, 0.0)
    wide_real = jnp.concatenate([psi[:high], beyond[:high]], axis=1)
    wide_imag = jnp.concatenate([psi[high:], beyond[high:]], axis=1)
    total_real, total_imag = gradient_sums(
        starts, wide_real, wide_imag, measured, probe, tables
    )
    total = jnp.concatenate([total_real, total_imag], axis=0) * (1.0 / measured.shape[0])
    mine = psi + total[:, :side] + coupling * (drawn - psi)
    rest = drawn - mine
    part[...] = mine
    want[...] = drawn
    send[:rows] = total[:, side:].astype(bf16)
    near[...] = rest
    send[rows:] = pack_edges(near, lines).astype(bf16)
    far[...] = total[:, side:]
    rim[...] = pack_edges(far, lines).astype(bf16)


def second_gradient(
    starts, inside, base, pull, spread, pair, beside, edges, two, measured, probe, tables, lines
):
    rows, side = base.shape
    groups = rows // lines
    smem = pl.BlockSpec(memory_space=pltpu.SMEM)
    vmem = pl.BlockSpec(memory_space=pltpu.VMEM)
    return pl.pallas_call(
        lambda *refs: second_kernel(lines, *refs),
        out_shape=[
            jax.ShapeDtypeStruct((rows, side), f32),
            jax.ShapeDtypeStruct((rows, side), f32),
            jax.ShapeDtypeStruct((rows + groups, side), bf16),
            jax.ShapeDtypeStruct((groups, side), bf16),
        ],
        in_specs=[smem] * 2 + [vmem] * 10,
        out_specs=[vmem] * 4,
        scratch_shapes=[pltpu.VMEM((rows, side), f32), pltpu.VMEM((rows, side), f32)],
        compiler_params=pltpu.CompilerParams(vmem_limit_bytes=32 * 1024 * 1024),
    )(starts, inside, base, pull, spread, pair, beside, edges, two, measured, probe, tables)


def close_kernel(lines, ends, part, want, pair, beside, two, rim, psi, parcel, plain, lined):
    rows, side = part.shape
    groups = rows // lines
    stride = lines + 2
    odd = ends[2] > 0
    up = jnp.where(odd, pair[...].astype(f32), beside[...].astype(f32))
    down = jnp.where(odd, beside[rows:].astype(f32), pair[rows:].astype(f32))
    settled = part[...] + up[:rows]
    psi[...] = settled
    lined[...] = want[...] - settled
    for r in range(lines):
        plain[pl.ds(r, groups, stride=stride), :] = lined[pl.ds(r, groups, stride=lines), :]
    lane = lax.broadcasted_iota(jnp.int32, (groups, side), 1)
    left = jnp.where(ends[0] > 0, up[rows:] - two[...].astype(f32), 0.0)
    right = jnp.where(ends[1] > 0, down - rim[...].astype(f32), 0.0)
    packed = jnp.where(lane % (2 * HALO) < HALO, left, right)
    plain[pl.ds(lines, groups, stride=stride), :] = packed
    plain[pl.ds(lines + 1, groups, stride=stride), :] = jnp.zeros((groups, side), f32)
    parcel[...] = plain[...].astype(bf16)


def close(ends, part, want, pair, beside, two, rim, lines):
    rows, side = part.shape
    groups = rows // lines
    smem = pl.BlockSpec(memory_space=pltpu.SMEM)
    vmem = pl.BlockSpec(memory_space=pltpu.VMEM)
    return pl.pallas_call(
        lambda *refs: close_kernel(lines, *refs),
        out_shape=[
            jax.ShapeDtypeStruct((rows, side), f32),
            jax.ShapeDtypeStruct((groups * (lines + 2), side), bf16),
        ],
        in_specs=[smem] + [vmem] * 6,
        out_specs=[vmem] * 2,
        scratch_shapes=[
            pltpu.VMEM((groups * (lines + 2), side), f32),
            pltpu.VMEM((rows, side), f32),
        ],
        compiler_params=pltpu.CompilerParams(vmem_limit_bytes=32 * 1024 * 1024),
    )(ends, part, want, pair, beside, two, rim)


def shear_kernel(scale, lines, wide_out, source, choice, out, plain, taps, result):
    channels = choice.shape[0]
    side = source.shape[1]
    pieces = source.shape[0] // channels
    span = 2 * side if wide_out else side
    plain[...] = source[...].astype(f32)
    if pieces > lines:
        packed = plain[pl.ds(lines, channels, stride=pieces), :]
    for r in range(lines):
        near = plain[pl.ds(r, channels, stride=pieces), :]
        edge = open_edges(packed, r) if pieces > lines else jnp.zeros_like(near)
        wide = jnp.concatenate([near, edge], axis=1).astype(bf16)
        for d in range(TAPS):
            moved = pltpu.roll(wide, (2 * side + HALO - d) % (2 * side), 1)[:, :span]
            taps[d * channels : (d + 1) * channels, r * span : (r + 1) * span] = moved
    summed = dot(choice[...], taps[...]) * scale
    given = lines + 2 if wide_out else lines
    for r in range(lines):
        result[pl.ds(r, channels, stride=given), :] = summed[:, r * span : r * span + side]
    if wide_out:
        lane = lax.broadcasted_iota(jnp.int32, (channels, side), 1)
        packed = jnp.zeros((channels, side), f32)
        for r in range(lines):
            part = summed[:, r * span + side : (r + 1) * span]
            part = pltpu.roll(part, (HALO + 2 * HALO * r) % side, 1)
            packed = jnp.where(lane // (2 * HALO) == r, part, packed)
        result[pl.ds(lines, channels, stride=given), :] = packed
        result[pl.ds(lines + 1, channels, stride=given), :] = jnp.zeros_like(packed)
    out[...] = result[...].astype(bf16)


def shear_sum(source, choice, scale, lines, wide_out):
    channels = choice.shape[0]
    side = source.shape[1]
    given = (lines + 2 if wide_out else lines) * channels
    span = 2 * side if wide_out else side
    vmem = pl.BlockSpec(memory_space=pltpu.VMEM)
    return pl.pallas_call(
        lambda *refs: shear_kernel(scale, lines, wide_out, *refs),
        out_shape=jax.ShapeDtypeStruct((given, side), bf16),
        in_specs=[vmem] * 2,
        out_specs=vmem,
        scratch_shapes=[
            pltpu.VMEM(source.shape, f32),
            pltpu.VMEM((TAPS * channels, lines * span), bf16),
            pltpu.VMEM((given, side), f32),
        ],
        compiler_params=pltpu.CompilerParams(vmem_limit_bytes=32 * 1024 * 1024),
    )(source, choice)


def back_kernel(scale, lines, source, choice, settled, out, psi, plain, taps, result, done):
    copy = pltpu.make_async_copy(settled, psi, done)
    copy.start()
    shear_kernel(scale, lines, False, source, choice, out, plain, taps, result)
    copy.wait()


def back_sum(source, choice, settled, scale, lines):
    channels = choice.shape[0]
    side = source.shape[1]
    vmem = pl.BlockSpec(memory_space=pltpu.VMEM)
    return pl.pallas_call(
        lambda *refs: back_kernel(scale, lines, *refs),
        out_shape=[
            jax.ShapeDtypeStruct((lines * channels, side), bf16),
            jax.ShapeDtypeStruct(settled.shape, f32),
        ],
        in_specs=[vmem] * 3,
        out_specs=[vmem, pl.BlockSpec(memory_space=pl.ANY)],
        scratch_shapes=[
            pltpu.VMEM(source.shape, f32),
            pltpu.VMEM((TAPS * channels, lines * side), bf16),
            pltpu.VMEM((lines * channels, side), f32),
            pltpu.SemaphoreType.DMA,
        ],
        compiler_params=pltpu.CompilerParams(vmem_limit_bytes=32 * 1024 * 1024),
    )(source, choice, settled)


def strip_move(value, by):
    length = lax.axis_size("strip")
    pairs = [(i, i + by) for i in range(length) if 0 <= i + by < length]
    return lax.ppermute(value, "strip", pairs)


def strip_swap(value, begin):
    pairs = []
    for i in range(begin, lax.axis_size("strip") - 1, 2):
        pairs += [(i, i + 1), (i + 1, i)]
    return lax.ppermute(value, "strip", pairs)


def regroup(value, groups):
    side = value.shape[-1]
    parcel = value.reshape(groups, value.shape[0] // (2 * groups), 2, side)
    return lax.all_to_all(parcel, "view", 0, 0, tiled=True).reshape(value.shape)


def per_device(slab, psi_start, dual, amplitudes, offsets, angles, probe):
    slices = lax.axis_size("view")
    own_slab = slab[0]
    shape = own_slab.shape
    psi = psi_start[0]
    own_dual = dual[0]
    measured = amplitudes[0]
    starts = offsets[0]
    root_scale = 1.0 / math.sqrt(slices)
    tables = dft_blocks(probe.shape[1])

    depth = jnp.arange(slices, dtype=jnp.int32)
    tilt = angles - HALO
    shift = (tilt[:, None] * (2 * depth[None, :] - slices + 1)) // slices
    tap = jnp.arange(TAPS, dtype=jnp.int32) - HALO
    choice_project = (
        (shift[:, None, :] == tap[None, :, None]).astype(bf16).reshape(slices, TAPS * slices)
    )
    choice_back = (
        (-shift.T[:, None, :] == tap[None, :, None]).astype(bf16).reshape(slices, TAPS * slices)
    )

    lines = shape[0] * shape[1] // slices
    place = lax.axis_index("strip")
    odd = place % 2
    inside = (place < lax.axis_size("strip") - 1).astype(jnp.int32)
    ends = jnp.stack([(place > 0).astype(jnp.int32), inside, odd])
    following = strip_move(psi, -1)
    lined = regroup(own_slab.reshape(lines * slices, shape[2]), slices)
    sums = shear_sum(lined, choice_project, root_scale, lines, True)
    sums, following = lax.optimization_barrier((sums, following))
    sums = regroup(sums, slices)
    spread = first_gradient(starts, psi, following, measured, probe, tables)
    base, pull, pair, beside, edges = between(ends[2:], sums, spread, psi, own_dual, lines)
    two = strip_move(edges, -2)
    beside = strip_swap(beside, 1)
    pair = strip_swap(pair, 0)
    part, want, send, rim = second_gradient(
        starts, ends[1:], base, pull, spread, pair, beside, edges, two, measured, probe, tables,
        lines,
    )
    two = strip_move(rim, 2)
    beside = strip_swap(send, 1)
    pair = strip_swap(send, 0)
    psi, parcel = close(ends, part, want, pair, beside, two, rim, lines)
    lined = regroup(parcel, slices)
    sums, psi = back_sum(lined, choice_back, psi, descent * root_scale, lines)
    psi = psi.reshape(shape)
    backward = regroup(sums, slices).reshape(shape).astype(f32)
    slab_new = (own_slab.astype(f32) - backward).astype(bf16)
    return (psi[None], slab_new[None])


def solution(mesh):
    return jax.shard_map(
        per_device,
        mesh=mesh,
        in_specs=(
            P("view", None, None, "strip"),
            P("view", None, None, "strip"),
            P("view", None, None, "strip"),
            P("view", "strip", None, None),
            P("view", "strip"),
            P(),
            P(),
        ),
        out_specs=(P("view", None, None, "strip"), P("view", None, None, "strip")),
        check_vma=False,
    )
```
